32 devices in a mesh: tm: 8 (over y, x, core), head: 4 (over z).
Axes of the slice: x: 2, y: 2, z: 4, core: 2. Of those that a mesh axis runs over, the one named last changes fastest.
Arguments:
- query_vectors: bfloat16 [8192, 4096], P('tm', 'head'), may hold values from -6 to 6
- key_vectors: bfloat16 [8192, 4096], P('tm', 'head'), may hold values from -0.125 to 0.125
- value_vectors: bfloat16 [8192, 4096], P('tm', 'head'), may hold values from -6 to 6
- grad_out: bfloat16 [8192, 4096], P('tm', 'head'), may hold values from -8 to 8
- out_weight: bfloat16 [4096, 4096], P('tm', 'head'), may hold values from -0.09375 to 0.09375
- periods: int32 [32], P('head'), may hold values from 1 to 128, as said below
- log_decay: float32 [32, 8192], P('head', 'tm'), may hold values from -0.1109375 to 0, as said below
Outputs:
- query_gradient: bfloat16 [8192, 4096], P('tm', 'head')
- key_gradient: bfloat16 [8192, 4096], P('tm', 'head')
- value_gradient: bfloat16 [8192, 4096], P('tm', 'head')
- grad_weight: float32 [4096, 4096], P('tm', 'head')
The draws below stay inside these ranges and needn't reach their ends.
Inputs may be any that keep to these rules, and one draw needn't show every extreme that they name: `periods`: some head has period 1 and some head period 128. `log_decay`: Negative.
All inputs are finite; a program needn't handle non-finite values.
Results may differ from the reference program's by a relative error of at most 0.023.
Values may be sent and summed in bfloat16 or wider, within the bound.
No kernel may reach another device: no remote copies, remote signals or barrier semaphores. Data moves between devices by JAX's collectives and lax.ppermute only.
A program may use at most 128 MiB of HBM per device.

```python
import math
import jax
import jax.numpy as jnp
from jax import lax

D = 4096
H = 32
DK = 128
BLK = 512
TOK_DEV = 1024
TOKENS = 8192


def draw_periods(key, part):
    base_key = jax.random.fold_in(key, 11)
    first_key, second_key = jax.random.split(base_key)
    periods = jax.random.randint(first_key, (H,), 1, 129)
    shuffled = jax.random.permutation(second_key, H)
    periods = periods.at[shuffled[0]].set(1)
    periods = periods.at[shuffled[1]].set(128)
    return periods.astype(jnp.int32)


def draw_log_decay(key, part):
    base_key = jax.random.fold_in(key, 23)
    split_keys = jax.random.split(base_key, 7)
    rapid_share = 0.5
    rapid = jax.random.uniform(split_keys[0], (H,)) < rapid_share
    span_len = jax.random.uniform(split_keys[1], (H,), minval=30.0, maxval=50.0)
    slow_rate = jax.random.uniform(split_keys[2], (H,), minval=0.05, maxval=0.25) * math.log(10.0) / TOKENS
    decay_factor = jnp.where(rapid, 1.0 / span_len, slow_rate)
    decay_spread = jax.random.uniform(split_keys[3], (H, TOKENS), minval=0.5, maxval=1.5)
    period_region = 2.0 ** jax.random.uniform(split_keys[4], (H, TOKENS // TOK_DEV), minval=-1.0, maxval=1.0)
    period_region = jnp.repeat(period_region, TOK_DEV, axis=1)
    window = min(128, TOKENS)
    starts = jax.random.randint(split_keys[5], (H, 2), 0, TOKENS - window + 1)
    decay_strength = jnp.log(jax.random.uniform(split_keys[6], (H, 2), minval=0.5, maxval=0.8)) / window
    positions = jnp.arange(TOKENS)
    inner_block = (positions[None, None, :] >= starts[:, :, None]) & (positions[None, None, :] < starts[:, :, None] + window)
    period_groups = jnp.sum(inner_block.astype(jnp.float32) * decay_strength[:, :, None], axis=1)
    return (-decay_factor[:, None] * decay_spread * period_region + period_groups).astype(jnp.float32)


def strengthened(entries, stream_key, source, target, parts, factor):
    owner, partner = [(jnp.arange(entries.shape[dim]) // (entries.shape[dim] // parts)).reshape([-1 if axis == dim else 1 for axis in range(entries.ndim)]) for dim in (source, target)]
    chosen = jax.random.permutation(stream_key, parts)[partner]
    strong = (owner == chosen) | (owner == (partner + parts // 2) % parts)
    return jnp.where(strong, factor * entries, entries)


def block_scale(stream_key, dims, pieces, least, top_value):
    def one(dim, parts):
        draws = jax.random.uniform(jax.random.fold_in(jax.random.fold_in(stream_key, 6), dim), (parts,), jnp.float32, least / len(pieces), top_value / len(pieces))
        return jnp.repeat(jnp.exp(draws), dims[dim] // parts).reshape((-1,) + (1,) * (len(dims) - dim - 1))

    level = one(*pieces[0])
    for cut in pieces[1:]:
        level = level * one(*cut)
    return level


def scatter_about(own_key, shape, scale, limit, pieces=(), held_as=jnp.bfloat16):
    entries = scale * jax.random.normal(own_key, shape, jnp.float32)
    if pieces:
        entries = entries * block_scale(own_key, shape, pieces, -0.22, 0.18)
    return jnp.clip(entries, -limit, limit).astype(held_as)


def bell_draw_with(rng, extent, width, most, pieces, heavy, kind=jnp.bfloat16):
    values = width * jax.random.normal(rng, extent, jnp.float32)
    if pieces:
        values = values * block_scale(rng, extent, pieces, -0.22, 0.18)
    return jnp.clip(strengthened(values, jax.random.fold_in(rng, 3), *heavy), -most, most).astype(kind)


def setup_inputs(seed: int = 0) -> dict:
    splits = jax.random.split(jax.random.key(seed), 8)
    return {
        "query_vectors": scatter_about(splits[0], (TOKENS, H * DK), 1.0, 6.0, ((0, 8), (1, 4))),
        "key_vectors": scatter_about(splits[1], (TOKENS, H * DK), 0.02, 0.125, ((0, 8), (1, 4))),
        "value_vectors": scatter_about(splits[2], (TOKENS, H * DK), 1.0, 6.0, ((0, 8), (1, 4))),
        "grad_out": bell_draw_with(splits[3], (TOKENS, D), 1.0, 8.0, ((0, 8), (1, 4)), (0, 1, 8, 2.0)),
        "out_weight": scatter_about(splits[4], (D, H * DK), D ** -0.5, 0.09375, ((0, 8), (1, 4))),
        "periods": draw_periods(jax.random.fold_in(splits[7], 71), 0),
        "log_decay": draw_log_decay(jax.random.fold_in(splits[7], 71), 0),
    }


def to_single_precision(tensor):
    return tensor.astype(jnp.float32)


def block_mask(cumul, update):
    span_len = cumul.shape[1]
    causal = jnp.arange(span_len)[:, None] >= jnp.arange(span_len)[None, :]
    spread = jnp.where(causal[None], cumul[:, :, None] - cumul[:, None, :], -jnp.inf)
    return jnp.exp(spread) * update[:, None, :]


def reference(query_vectors, key_vectors, value_vectors, grad_out, out_weight, periods, log_decay):
    grad_mixed = jnp.dot(grad_out, out_weight, preferred_element_type=jnp.float32).astype(jnp.bfloat16)
    positions = jnp.arange(TOKENS, dtype=jnp.int32)
    update = (positions[None, :] % periods[:, None] == 0).astype(jnp.float32)
    step_log = update * periods[:, None].astype(jnp.float32) * log_decay
    block_count = TOKENS // BLK
    cumulative = jnp.cumsum(step_log.reshape(H, block_count, BLK), axis=2).transpose(1, 0, 2)
    updates = update.reshape(H, block_count, BLK).transpose(1, 0, 2)

    def blocked(tensor):
        return tensor.reshape(block_count, BLK, H, DK)

    query_blocks = blocked(query_vectors)
    key_blocks = blocked(key_vectors)
    value_blocks = blocked(value_vectors)
    grad_blocks = blocked(grad_mixed)
    zero_state = jnp.zeros((H, DK, DK), jnp.float32)

    def forward(running, section):
        key_matrix, value_matrix, cumul, update_rows = section
        block_total = cumul[:, -1]
        factor = update_rows * jnp.exp(block_total[:, None] - cumul)
        decay_scaled = (to_single_precision(key_matrix) * factor.T[:, :, None]).astype(jnp.bfloat16)
        outer_product = jnp.einsum('ptz,ptb->tzb', to_single_precision(decay_scaled), to_single_precision(value_matrix))
        return jnp.exp(block_total)[:, None, None] * running + outer_product, running

    _, starts = lax.scan(forward, zero_state, (key_blocks, value_blocks, cumulative, updates))

    def backward(carried_in, section):
        query_matrix, gradient_rows, cumul = section
        decay_scaled = (to_single_precision(query_matrix) * jnp.exp(cumul).T[:, :, None]).astype(jnp.bfloat16)
        outer_product = jnp.einsum('yop,yoj->opj', to_single_precision(decay_scaled), to_single_precision(gradient_rows))
        return jnp.exp(cumul[:, -1])[:, None, None] * carried_in + outer_product, carried_in

    _, finishes = lax.scan(backward, zero_state, (query_blocks, grad_blocks, cumulative), reverse=True)

    def every_output(section):
        query_matrix, key_matrix, value_matrix, gradient_rows, cumul, update_rows, state_start, finish = section
        decay_mask = block_mask(cumul, update_rows)
        scores = jnp.einsum('thk,shk->hts', to_single_precision(query_matrix), to_single_precision(key_matrix))
        reversed_blocks = jnp.einsum('thv,shv->hts', to_single_precision(gradient_rows), to_single_precision(value_matrix))
        projection_weight = (scores * decay_mask).astype(jnp.bfloat16)
        reversed_blocks = (reversed_blocks * decay_mask).astype(jnp.bfloat16)
        state_reduced = state_start.astype(jnp.bfloat16)
        carry_reduced = finish.astype(jnp.bfloat16)
        incoming_gradient = jnp.exp(cumul).T[:, :, None]
        outgoing_gradient = (update_rows * jnp.exp(cumul[:, -1][:, None] - cumul)).T[:, :, None]
        within = jnp.einsum('hts,shv->thv', to_single_precision(projection_weight), to_single_precision(value_matrix))
        carried_state = jnp.einsum('qml,mla->qma', to_single_precision(query_matrix), to_single_precision(state_reduced))
        mixed = (within + incoming_gradient * carried_state).astype(jnp.bfloat16)
        query_gradient = jnp.einsum('gea,agq->egq', to_single_precision(reversed_blocks), to_single_precision(key_matrix)) + incoming_gradient * jnp.einsum('sba,bda->sbd', to_single_precision(gradient_rows), to_single_precision(state_reduced))
        key_gradient = jnp.einsum('rwy,wre->yre', to_single_precision(reversed_blocks), to_single_precision(query_matrix)) + outgoing_gradient * jnp.einsum('wqx,qgx->wqg', to_single_precision(value_matrix), to_single_precision(carry_reduced))
        value_gradient = jnp.einsum('kyp,ykb->pkb', to_single_precision(projection_weight), to_single_precision(gradient_rows)) + outgoing_gradient * jnp.einsum('imx,mxd->imd', to_single_precision(key_matrix), to_single_precision(carry_reduced))
        return mixed, query_gradient.astype(jnp.bfloat16), key_gradient.astype(jnp.bfloat16), value_gradient.astype(jnp.bfloat16)

    sections = (query_blocks, key_blocks, value_blocks, grad_blocks, cumulative, updates, starts, finishes)
    mixed, query_gradient, key_gradient, value_gradient = lax.map(every_output, sections)
    mixed = mixed.reshape(TOKENS, H * DK)
    grad_weight = jnp.dot(grad_out.T, mixed, preferred_element_type=jnp.float32)
    return (query_gradient.reshape(TOKENS, H * DK), key_gradient.reshape(TOKENS, H * DK), value_gradient.reshape(TOKENS, H * DK), grad_weight)
```

```python
import functools
import math

import jax
import jax.numpy as jnp
from jax import lax
from jax.experimental import pallas as pl
from jax.experimental.pallas import tpu as pltpu
from jax.sharding import PartitionSpec as P

DK = 128
BLK = 512
CHUNKS = 2
LOG2E = math.log2(math.e)
FAR = 1e30
F32 = jnp.float32
BF16 = jnp.bfloat16
PARAMS = pltpu.CompilerParams(vmem_limit_bytes=48 * 1024 * 1024)


def dot(a, b, da=1, db=0):
    return lax.dot_general(a, b, (((da,), (db,)), ((), ())), preferred_element_type=F32)


def cost(flops, moved):
    return pl.CostEstimate(flops=flops, bytes_accessed=moved, transcendentals=0)


def state_kernel(col, k, v, parts, local):
    state = jnp.zeros((DK, DK), F32)
    for b in range(parts.shape[1]):
        rows = pl.ds(b * BLK, BLK)
        scaled = (k[rows, :].astype(F32) * col[0, rows, 1:2]).astype(BF16)
        part = dot(scaled, v[rows, :], 0, 0)
        parts[0, b] = part
        state = state * col[0, pl.ds(b * BLK + BLK - 1, 1), 2:3] + part
    local[0] = state


def tiles(half):
    return ((0, 0), (1, 0), (1, 1))


def mask_tile(col, row, t, s, half, diagonal):
    spread = jnp.exp2(col[0, pl.ds(t, half), 0:1] - row[0, 0:1, pl.ds(s, half)])
    if diagonal:
        shape = (half, half)
        causal = lax.broadcasted_iota(jnp.int32, shape, 0) >= lax.broadcasted_iota(
            jnp.int32, shape, 1
        )
        spread = jnp.where(causal, spread, 0.0)
    return spread


def within_kernel(col, row, q, k, v, weights, within):
    half = BLK // 2
    for b in range(weights.shape[1]):
        sums = [None, None]
        for n, (i, j) in enumerate(tiles(half)):
            t, s = b * BLK + i * half, b * BLK + j * half
            scores = dot(q[pl.ds(t, half), :], k[pl.ds(s, half), :], 1, 1)
            tile = (scores * mask_tile(col, row, t, s, half, i == j)).astype(BF16)
            weights[0, b, n] = tile
            part = dot(tile, v[pl.ds(s, half), :])
            sums[i] = part if sums[i] is None else sums[i] + part
        for i in range(2):
            within[pl.ds(b * BLK + i * half, half), :] = sums[i]


def mixed_kernel(col, q, within, parts, start, mixed, states):
    state = start[0]
    for b in range(parts.shape[1]):
        rows = pl.ds(b * BLK, BLK)
        small = state.astype(BF16)
        states[0, b] = small
        carried = dot(q[rows, :], small)
        mixed[rows, :] = (within[rows, :] + col[0, rows, 2:3] * carried).astype(BF16)
        state = state * col[0, pl.ds(b * BLK + BLK - 1, 1), 2:3] + parts[0, b]


def grad_kernel(col, q, early, last, weight, e, parts, local):
    rows_all = early[...] + dot(last[...], weight[...])
    e[...] = rows_all.astype(BF16)
    for h in range(parts.shape[0]):
        lanes = pl.ds(h * DK, DK)
        state = jnp.zeros((DK, DK), F32)
        for b in reversed(range(parts.shape[1])):
            rows = pl.ds(b * BLK, BLK)
            scaled = (q[rows, lanes].astype(F32) * col[h, rows, 2:3]).astype(BF16)
            part = dot(scaled, e[rows, lanes], 0, 0)
            parts[h, b] = part
            state = state * col[h, pl.ds(b * BLK + BLK - 1, 1), 2:3] + part
        local[h] = state


def back_kernel(col, row, q, k, v, e, weights, states, dq, dk, dv):
    half = BLK // 2
    for b in range(weights.shape[1]):
        sums = [[None, None] for _ in range(3)]

        def add(which, at, part):
            old = sums[which][at]
            sums[which][at] = part if old is None else old + part

        for n, (i, j) in enumerate(tiles(half)):
            t, s = b * BLK + i * half, b * BLK + j * half
            at_t, at_s = pl.ds(t, half), pl.ds(s, half)
            raw = dot(e[at_t, :], v[at_s, :], 1, 1)
            tile = (raw * mask_tile(col, row, t, s, half, i == j)).astype(BF16)
            add(0, i, dot(tile, k[at_s, :]))
            add(1, j, dot(tile, q[at_t, :], 0, 0))
            add(2, j, dot(weights[0, b, n], e[at_t, :], 0, 0))
        for i in range(2):
            rows = pl.ds(b * BLK + i * half, half)
            carried = dot(e[rows, :], states[0, b], 1, 1)
            dq[rows, :] = (sums[0][i] + col[0, rows, 2:3] * carried).astype(BF16)
            dk[rows, :] = sums[1][i].astype(BF16)
            dv[rows, :] = sums[2][i].astype(BF16)


def finish_kernel(col, k, v, dk_part, dv_part, parts, finish, dk, dv):
    state = finish[0]
    for b in reversed(range(parts.shape[1])):
        rows = pl.ds(b * BLK, BLK)
        small = state.astype(BF16)
        factor = col[0, rows, 1:2]
        dk[rows, :] = (dk_part[rows, :].astype(F32) + factor * dot(v[rows, :], small, 1, 1)).astype(
            BF16
        )
        dv[rows, :] = (dv_part[rows, :].astype(F32) + factor * dot(k[rows, :], small)).astype(BF16)
        state = state * col[0, pl.ds(b * BLK + BLK - 1, 1), 2:3] + parts[0, b]


def log2_of(count):
    bits = count.bit_length() - 1
    assert 1 << bits == count
    return bits


def scan_states(total, decay, reverse, decays):
    count, place = lax.axis_size("tm"), lax.axis_index("tm")
    heads = total.shape[0]
    reached, across, own = jnp.zeros_like(total), jnp.ones_like(decay), decay
    seen = []
    for bit in range(log2_of(count)):
        perm = [(i, i ^ (1 << bit)) for i in range(count)]
        sent = total.astype(BF16)
        if decays is None:
            high = own.astype(BF16)
            low = (own - high.astype(F32)).astype(BF16)
            pair = jnp.concatenate(
                [jnp.broadcast_to(x[:, None, None], (heads, 8, DK)) for x in (high, low)], axis=1
            )
            got = lax.ppermute(jnp.concatenate([sent, pair], axis=1), "tm", perm)
            other = got[:, DK, 0].astype(F32) + got[:, DK + 8, 0].astype(F32)
            got = got[:, :DK].astype(F32)
        else:
            got = lax.ppermute(sent, "tm", perm).astype(F32)
            other = decays[bit]
        seen.append(other)
        upper = (place >> bit) & 1
        takes = (upper == 1) != reverse
        reached = jnp.where(takes, reached + across[:, None, None] * got, reached)
        across = jnp.where(takes, across * other, across)
        total = jnp.where(
            takes, total + own[:, None, None] * got, got + other[:, None, None] * total
        )
        own = own * other
    return reached, seen


def block_order(size):
    return [sorted(range(size), key=lambda q: (abs(p - q), p ^ q)) for p in range(size)]


def line_gather(pieces):
    size = lax.axis_size("head")
    have = {}
    left, right = list(pieces), list(pieces)
    for step in range(1, size):
        to_left = [(p, p - 1) for p in range(1, size) if p + step - 1 < size]
        to_right = [(p, p + 1) for p in range(size - 1) if p - step + 1 >= 0]
        for c in range(len(pieces)):
            left[c] = lax.ppermute(left[c], "head", to_left)
            right[c] = lax.ppermute(right[c], "head", to_right)
            have[(step, c)] = left[c]
            have[(-step, c)] = right[c]
    for c, piece in enumerate(pieces):
        have[(0, c)] = piece
    return have


def pick(by_plane, make):
    plane = lax.axis_index("head")
    keys = sorted(set(by_plane))
    out = make(keys[0])
    for key in keys[1:]:
        here = functools.reduce(
            jnp.logical_or, [plane == p for p, own in enumerate(by_plane) if own == key]
        )
        out = jnp.where(here, make(key), out)
    return out


def reduce_block(part, targets, flips):
    count, size = lax.axis_size("tm"), lax.axis_size("head")
    group = part.shape[0]
    place = lax.axis_index("tm")
    held = part
    width = group
    while width > 1:
        width //= 2
        perm = [(i, i ^ width) for i in range(count)]
        upper = (place // width) % 2 == 1
        first, second = held[:width], held[width:]
        got = lax.ppermute(jnp.where(upper, first, second), "tm", perm)
        held = (jnp.where(upper, second, first).astype(F32) + got.astype(F32)).astype(BF16)
    held = held[0]
    out = []
    span = held.shape[1] // len(flips)
    for n, order in enumerate(flips):
        now = held[:, n * span : (n + 1) * span]
        done = 0
        for bit in order:
            perm = []
            for i in range(count):
                for p in range(size):
                    far = (i // group) ^ targets[p]
                    if far & bit and not far & done:
                        perm.append((i * size + p, (i ^ (bit * group)) * size + p))
            got = lax.ppermute(now.astype(BF16), ("tm", "head"), perm)
            now = now.astype(F32) + got.astype(F32)
            done |= bit
        out.append(now)
    return jnp.concatenate(out, axis=1) if len(out) > 1 else out[0]


def per_device(query, key, value, grad_out, out_weight, periods, log_decay):
    tok, width = query.shape
    heads = periods.shape[0]
    blocks = tok // BLK
    count, size = lax.axis_size("tm"), lax.axis_size("head")
    group = count // size
    plane = lax.axis_index("head")
    place = lax.axis_index("tm")
    sub = grad_out.shape[1] // group
    piece = sub // CHUNKS

    split = grad_out.reshape(tok, group, CHUNKS, piece)
    pieces = [split[:, :, c].reshape(tok, group * piece) for c in range(CHUNKS)]
    have = line_gather(pieces)
    full_weight = lax.all_gather(out_weight, "tm", axis=0, tiled=True)

    positions = place * tok + jnp.arange(tok, dtype=jnp.int32)
    update = positions[None, :] % periods[:, None] == 0
    step_log = jnp.where(update, periods[:, None].astype(F32) * log_decay, 0.0)
    cumul = jnp.cumsum(step_log.reshape(heads, blocks, BLK), axis=2)
    totals = cumul[:, :, -1]
    key_factor = jnp.where(
        update.reshape(heads, blocks, BLK), jnp.exp(totals[:, :, None] - cumul), 0.0
    ).reshape(heads, tok)
    cumul = cumul.reshape(heads, tok)
    scaled_log = cumul * LOG2E
    col = jnp.stack([scaled_log, key_factor, jnp.exp(cumul)], axis=2)
    row = jnp.where(update, scaled_log, FAR)[:, None, :]
    decay = jnp.exp(jnp.sum(totals, axis=1))

    half = BLK // 2
    head_rows = pl.BlockSpec((tok, DK), lambda h: (0, h))
    cols = pl.BlockSpec((1, tok, 3), lambda h: (h, 0, 0))
    rows = pl.BlockSpec((1, 1, tok), lambda h: (h, 0, 0))
    block_states = pl.BlockSpec((1, blocks, DK, DK), lambda h: (h, 0, 0, 0))
    one_state = pl.BlockSpec((1, DK, DK), lambda h: (h, 0, 0))
    tiles_spec = pl.BlockSpec((1, blocks, 3, half, half), lambda h: (h, 0, 0, 0, 0))
    shape = jax.ShapeDtypeStruct
    states_f32 = shape((heads, blocks, DK, DK), F32)
    states_bf16 = shape((heads, blocks, DK, DK), BF16)
    state_f32 = shape((heads, DK, DK), F32)
    rows_bf16 = shape((tok, width), BF16)
    pair_flops = 2 * tok * BLK * width

    fwd_parts, fwd_local = pl.pallas_call(
        state_kernel,
        grid=(heads,),
        in_specs=[cols, head_rows, head_rows],
        out_specs=[block_states, one_state],
        out_shape=[states_f32, state_f32],
        compiler_params=PARAMS,
        cost_estimate=cost(2 * tok * DK * width, 12 * tok * width),
        name="block_states",
    )(col, key, value)
    state_in, decays = scan_states(fwd_local, decay, False, None)
    weights, within = pl.pallas_call(
        within_kernel,
        grid=(heads,),
        in_specs=[cols, rows, head_rows, head_rows, head_rows],
        out_specs=[tiles_spec, head_rows],
        out_shape=[shape((heads, blocks, 3, half, half), BF16), shape((tok, width), F32)],
        compiler_params=PARAMS,
        cost_estimate=cost(3 * pair_flops, 20 * tok * width),
        name="pair_weights",
    )(col, row, query, key, value)
    mixed, states = pl.pallas_call(
        mixed_kernel,
        grid=(heads,),
        in_specs=[cols, head_rows, head_rows, block_states, one_state],
        out_specs=[head_rows, block_states],
        out_shape=[rows_bf16, states_bf16],
        compiler_params=PARAMS,
        cost_estimate=cost(2 * tok * DK * width, 12 * tok * width),
        name="mixed_rows",
    )(col, query, within, fwd_parts, state_in)

    order = block_order(size)
    weight_parts = full_weight.reshape(size, group, CHUNKS, piece, width)
    early = None
    sums = []
    bits = [1 << b for b in range(log2_of(size))]
    for s in range(size):
        targets = [order[p][s] for p in range(size)]
        at = pick(targets, lambda q: jnp.int32(q))
        final = s == size - 1
        for c in range(CHUNKS):
            block = pick([q - p for p, q in enumerate(targets)], lambda k: have[(k, c)])
            weight = lax.dynamic_slice(
                weight_parts, (at, 0, c, 0, 0), (1, group, 1, piece, width)
            ).reshape(group * piece, width)
            if final and c == CHUNKS - 1:
                last, last_weight = block, weight
            else:
                part = jnp.dot(block, weight, preferred_element_type=F32)
                early = part if early is None else early + part
            product = dot(block, mixed, 0, 0).astype(BF16).reshape(group, piece, width)
            flips = [bits[::-1], bits] if final else [bits[::-1] if s % 2 else bits]
            done = reduce_block(product, targets, flips)
            mine = pick(targets, lambda q: jnp.int32(q)) == place // group
            sums.append((c, mine, done))
    grad_weight = []
    for c in range(CHUNKS):
        out = None
        for chunk, mine, done in sums:
            if chunk == c:
                out = done.astype(F32) if out is None else jnp.where(mine, done.astype(F32), out)
        grad_weight.append(out)
    grad_weight = jnp.concatenate(grad_weight, axis=0)

    two = 2 if heads % 2 == 0 else 1
    wide = pl.BlockSpec((tok, two * DK), lambda h: (0, h))
    e, back_parts, back_local = pl.pallas_call(
        grad_kernel,
        grid=(heads // two,),
        in_specs=[
            pl.BlockSpec((two, tok, 3), lambda h: (h, 0, 0)),
            wide,
            wide,
            pl.BlockSpec(last.shape, lambda h: (0, 0)),
            pl.BlockSpec((last.shape[1], two * DK), lambda h: (0, h)),
        ],
        out_specs=[
            wide,
            pl.BlockSpec((two, blocks, DK, DK), lambda h: (h, 0, 0, 0)),
            pl.BlockSpec((two, DK, DK), lambda h: (h, 0, 0)),
        ],
        out_shape=[rows_bf16, states_f32, state_f32],
        compiler_params=PARAMS,
        cost_estimate=cost(2 * tok * last.shape[1] * width, 16 * tok * width),
        name="grad_mixed_rows",
    )(col, query, early, last, last_weight)
    grad_in, _ = scan_states(back_local, decay, True, decays)
    dq, dk_part, dv_part = pl.pallas_call(
        back_kernel,
        grid=(heads,),
        in_specs=[cols, rows] + [head_rows] * 4 + [tiles_spec, block_states],
        out_specs=[head_rows] * 3,
        out_shape=[rows_bf16] * 3,
        compiler_params=PARAMS,
        cost_estimate=cost(5 * pair_flops, 24 * tok * width),
        name="block_gradients",
    )(col, row, query, key, value, e, weights, states)
    dk, dv = pl.pallas_call(
        finish_kernel,
        grid=(heads,),
        in_specs=[cols] + [head_rows] * 4 + [block_states, one_state],
        out_specs=[head_rows] * 2,
        out_shape=[rows_bf16] * 2,
        compiler_params=PARAMS,
        cost_estimate=cost(4 * tok * DK * width, 16 * tok * width),
        name="carried_gradients",
    )(col, key, value, dk_part, dv_part, back_parts, grad_in)
    return dq, dk, dv, grad_weight


def solution(mesh):
    both = P("tm", "head")
    return jax.shard_map(
        per_device,
        mesh=mesh,
        in_specs=(both, both, both, both, both, P("head"), P("head", "tm")),
        out_specs=(both, both, both, both),
        check_vma=False,
    )
```

```python
import functools
import math

import jax
import jax.numpy as jnp
from jax import lax
from jax.experimental import pallas as pl
from jax.experimental.pallas import tpu as pltpu
from jax.sharding import PartitionSpec as P

DK = 128
BLK = 512
LOG2E = math.log2(math.e)
FAR = 1e30
F32 = jnp.float32
BF16 = jnp.bfloat16
PARAMS = pltpu.CompilerParams(vmem_limit_bytes=60 * 1024 * 1024)


def dot(a, b, da=1, db=0):
    return lax.dot_general(a, b, (((da,), (db,)), ((), ())), preferred_element_type=F32)


LIGHT = pl.CostEstimate(flops=1, bytes_accessed=1, transcendentals=0)


def factors_kernel(offset, periods, log_decay, out):
    shape = log_decay.shape
    lane = lax.broadcasted_iota(jnp.int32, shape, 1)
    period = jnp.broadcast_to(periods[...], shape)
    update = lax.rem(offset[0] + lane, period) == 0
    cumul = jnp.where(update, period.astype(F32) * log_decay[...], 0.0)
    place = lane % BLK
    step = 1
    while step < BLK:
        cumul = cumul + jnp.where(place >= step, pltpu.roll(cumul, step, 1), 0.0)
        step *= 2
    left = [cumul[:, t : t + BLK] for t in range(0, shape[1], BLK)]
    left = jnp.concatenate([x[:, BLK - 1 : BLK] - x for x in left], axis=1)
    scaled = cumul * LOG2E
    rows = (
        scaled,
        jnp.where(update, jnp.exp(left), 0.0),
        jnp.exp(cumul),
        jnp.where(update, scaled, FAR),
    )
    out[...] = jnp.zeros(out.shape, F32)
    for h in range(shape[0]):
        for r, x in enumerate(rows):
            out[h, r : r + 1, :] = x[h : h + 1, :]


def columns(factors, h=0):
    return jnp.transpose(factors[h])


def pack_decay(sent, h, decay):
    high = decay.astype(BF16)
    low = (decay - high.astype(F32)).astype(BF16)
    sent[h, DK : DK + 16, :] = jnp.broadcast_to(high, (16, DK))
    sent[h, DK + 16 : DK + 32, :] = jnp.broadcast_to(low, (16, DK))


def lanes_of(h):
    return slice(h * DK, (h + 1) * DK)


def state_kernel(factors, k, v, parts, local, own, sent):
    for h in range(parts.shape[0]):
        col, lanes = columns(factors, h), lanes_of(h)
        state = jnp.zeros((DK, DK), F32)
        decay = jnp.ones((1, 1), F32)
        for b in range(parts.shape[1]):
            at, end = b * BLK, (b + 1) * BLK
            scaled = (k[at:end, lanes].astype(F32) * col[at:end, 1:2]).astype(BF16)
            part = dot(scaled, v[at:end, lanes], 0, 0)
            parts[h, b] = part
            fade = col[end - 1 : end, 2:3]
            state = state * fade + part
            decay = decay * fade
        local[h] = state
        own[h] = jnp.broadcast_to(decay, (8, DK))
        sent[h, 0:DK, :] = state.astype(BF16)
        pack_decay(sent, h, jnp.broadcast_to(decay, (1, DK)))


def add_kernel(a, b, out):
    out[...] = (a[...].astype(F32) + b[...].astype(F32)).astype(BF16)


def total_block(refs):
    block = refs[0][...]
    for other in refs[1:]:
        block = block + other[...]
    return block


def halves_kernel(core, *refs):
    *inputs, mixed, sent, kept = refs
    total = dot(total_block(inputs), mixed[...], 0, 0).astype(BF16)

    @pl.when(pl.program_id(0) == 0)
    def _():
        sent[...] = total

    @pl.when(pl.program_id(0) == 1)
    def _():
        kept[...] = total


def rows_kernel(counts, order, *refs):
    inputs, mixed, out = refs[: sum(counts)], refs[sum(counts)], refs[-1]
    at = 0
    for n, many in enumerate(counts):
        mine = inputs[at : at + many]
        at += many

        @pl.when(pl.program_id(0) == n)
        def _(mine=mine):
            if mine:
                out[...] = dot(total_block(mine), mixed[...], 0, 0).astype(BF16)
            else:
                out[...] = jnp.zeros(out.shape, BF16)


def masks(col, row, at):
    half = BLK // 2
    out = []
    for start in (0, half):
        spread = jnp.exp2(
            col[at + start : at + BLK, 0:1] - row[:, at + start : at + start + half]
        )
        size = (BLK - start, half)
        causal = lax.broadcasted_iota(jnp.int32, size, 0) >= lax.broadcasted_iota(
            jnp.int32, size, 1
        )
        out.append(jnp.where(causal, spread, 0.0))
    return out


def within_kernel(factors, q, k, v, weights, within):
    half = BLK // 2
    for h in range(weights.shape[0]):
        col, lanes = columns(factors, h), lanes_of(h)
        for b in range(weights.shape[1]):
            at, mid, end = b * BLK, b * BLK + half, (b + 1) * BLK
            first, second = masks(col, factors[h, 3:4, :], at)
            first = (dot(q[at:end, lanes], k[at:mid, lanes], 1, 1) * first).astype(BF16)
            second = (dot(q[mid:end, lanes], k[mid:end, lanes], 1, 1) * second).astype(BF16)
            weights[h, b, 0:BLK, :] = first
            weights[h, b, BLK : BLK + half, :] = second
            part = dot(first, v[at:mid, lanes])
            within[at:mid, lanes] = part[:half]
            within[mid:end, lanes] = part[half:] + dot(second, v[mid:end, lanes])


def mixed_kernel(factors, q, within, parts, start, mixed, states):
    for h in range(parts.shape[0]):
        col, lanes = columns(factors, h), lanes_of(h)
        state = start[h]
        for b in range(parts.shape[1]):
            at, end = b * BLK, (b + 1) * BLK
            small = state.astype(BF16)
            states[h, b] = small
            carried = dot(q[at:end, lanes], small)
            total = within[at:end, lanes] + col[at:end, 2:3] * carried
            mixed[at:end, lanes] = total.astype(BF16)
            state = state * col[end - 1 : end, 2:3] + parts[h, b]


def block_products(counts, rows, blocks):
    total = None
    at = 0
    for n, many in enumerate(counts):
        block = blocks[at][...]
        for other in blocks[at + 1 : at + many]:
            block = block + other[...]
        at += many
        part = dot(block, rows(n))
        total = part if total is None else total + part
    return total


def early_kernel(counts, order, *refs):
    *inputs, out = refs
    shards, inputs = inputs[-len(counts) :], inputs[: -len(counts)]
    before, blocks = (inputs[0], inputs[1:]) if len(inputs) > sum(counts) else (None, inputs)
    total = block_products(counts, lambda n: shards[n][...], blocks)
    out[...] = total if before is None else before[...] + total


def grad_kernel(counts, order, factors, q, early, *refs):
    *blocks, weight, e, parts, local, sent = refs
    e[...] = (early[...] + block_products(counts, lambda n: weight[...], blocks)).astype(BF16)
    for h in range(parts.shape[0]):
        col, lanes = columns(factors, h), lanes_of(h)
        state = jnp.zeros((DK, DK), F32)
        for b in reversed(range(parts.shape[1])):
            at, end = b * BLK, (b + 1) * BLK
            scaled = (q[at:end, lanes].astype(F32) * col[at:end, 2:3]).astype(BF16)
            part = dot(scaled, e[at:end, lanes], 0, 0)
            parts[h, b] = part
            state = state * col[end - 1 : end, 2:3] + part
        local[h] = state
        sent[h] = state.astype(BF16)


def back_kernel(factors, q, k, v, e, weights, states, dq, dk, dv):
    half = BLK // 2
    for h in range(weights.shape[0]):
        col, lanes = columns(factors, h), lanes_of(h)
        first, second = masks(col, factors[h, 3:4, :], 0)
        first = (dot(e[:, lanes], v[0:half, lanes], 1, 1) * first).astype(BF16)
        second = (dot(e[half:BLK, lanes], v[half:BLK, lanes], 1, 1) * second).astype(BF16)
        carried = col[:, 2:3] * dot(e[:, lanes], states[h, 0], 1, 1) + dot(first, k[0:half, lanes])
        dq[0:half, lanes] = carried[:half].astype(BF16)
        more = dot(second, k[half:BLK, lanes])
        dq[half:BLK, lanes] = (carried[half:] + more).astype(BF16)
        dk[0:half, lanes] = dot(first, q[:, lanes], 0, 0).astype(BF16)
        dk[half:BLK, lanes] = dot(second, q[half:BLK, lanes], 0, 0).astype(BF16)
        dv[0:half, lanes] = dot(weights[h, 0, 0:BLK, :], e[:, lanes], 0, 0).astype(BF16)
        tail = weights[h, 0, BLK : BLK + half, :]
        dv[half:BLK, lanes] = dot(tail, e[half:BLK, lanes], 0, 0).astype(BF16)


def finish_kernel(factors, k, v, dk_part, dv_part, parts, finish, dk, dv):
    for h in range(finish.shape[0]):
        col, lanes = columns(factors, h), lanes_of(h)
        state = finish[h]
        for b in reversed(range(parts.shape[1])):
            at, end = b * BLK, (b + 1) * BLK
            small = state.astype(BF16)
            factor = col[at:end, 1:2]
            more = factor * dot(v[at:end, lanes], small, 1, 1)
            dk[at:end, lanes] = (dk_part[at:end, lanes].astype(F32) + more).astype(BF16)
            more = factor * dot(k[at:end, lanes], small)
            dv[at:end, lanes] = (dv_part[at:end, lanes].astype(F32) + more).astype(BF16)
            state = state * col[end - 1 : end, 2:3] + parts[h, b]


def log2_of(count):
    bits = count.bit_length() - 1
    assert 1 << bits == count
    return bits


def tie(value, *after):
    return lax.optimization_barrier((value,) + after)[0] if after else value


def call(kernel, *args, out, name, prefetch=0):
    return pl.pallas_call(
        kernel,
        grid_spec=pltpu.PrefetchScalarGridSpec(
            num_scalar_prefetch=prefetch,
            grid=(1,),
            in_specs=[pl.BlockSpec(x.shape, lambda *_, r=x.ndim: (0,) * r) for x in args[prefetch:]],
            out_specs=[pl.BlockSpec(x.shape, lambda *_, r=len(x.shape): (0,) * r) for x in out],
        ),
        out_shape=out,
        compiler_params=PARAMS,
        cost_estimate=LIGHT,
        name=name,
    )(*args)


def with_decay(state, decay):
    high = decay.astype(BF16)
    low = (decay - high.astype(F32)).astype(BF16)
    pair = [jnp.broadcast_to(x, x.shape[:1] + (16, DK)) for x in (high, low)]
    return jnp.concatenate([state.astype(BF16)] + pair, axis=1)


def decay_of(got):
    return got[:, DK : DK + 1, :].astype(F32) + got[:, DK + 16 : DK + 17, :].astype(F32)


class Scan:
    def __init__(self, total, own, sent, reverse, known=None):
        self.total, self.own, self.sent, self.reverse = total, own, sent, reverse
        self.first, self.known = known is None, known or {}

    def permute(self, value, mask):
        count = lax.axis_size("tm")
        return lax.ppermute(value, "tm", [(i, i ^ mask) for i in range(count)])

    def send_pair(self):
        self.got = self.permute(self.sent, 1)

    def take_pair(self, *after):
        got = tie(self.got, *after)
        if self.first:
            self.known[0] = decay_of(got)
        other = self.known[0]
        came = got[:, :DK].astype(F32)
        upper = lax.axis_index("tm") % 2 == 1
        self.takes = upper != self.reverse
        self.near, self.across = came, self.own
        here = jnp.where(self.takes, self.own, 1.0) * came
        self.pair = here + jnp.where(self.takes, 1.0, other) * self.total
        return self.pair

    def send_all(self):
        pairs = lax.axis_size("tm") // 2
        if self.first:
            sent = with_decay(self.pair, self.own * self.known[0])
        else:
            sent = self.pair.astype(BF16)
        self.all = {m: self.permute(sent, 2 * m) for m in range(1, pairs)}

    def take_all(self, *after):
        mine = lax.axis_index("tm") // 2
        got = {m: tie(x, *after) for m, x in self.all.items()}
        if self.first:
            self.known.update({m: decay_of(x) for m, x in got.items()})
        before = (lambda a, b: a > b) if self.reverse else (lambda a, b: a < b)
        state = None
        for m, x in got.items():
            weight = jnp.where(before(mine ^ m, mine), 1.0, 0.0)
            for n in got:
                if n != m:
                    between = before(mine ^ m, mine ^ n) & before(mine ^ n, mine)
                    weight = weight * jnp.where(between, self.known[n], 1.0)
            part = weight * x[:, :DK].astype(F32)
            state = part if state is None else state + part
        other = jnp.where(self.takes, self.known[0], 1.0)
        return other * state + jnp.where(self.takes, self.near, 0.0)


def block_order(size):
    return [sorted(range(size), key=lambda q: (abs(p - q), p ^ q)) for p in range(size)]


def pick(by_plane, make):
    plane = lax.axis_index("head")
    keys = sorted(set(by_plane))
    out = make(keys[0])
    for key in keys[1:]:
        here = functools.reduce(
            jnp.logical_or, [plane == p for p, own in enumerate(by_plane) if own == key]
        )
        out = jnp.where(here, make(key), out)
    return out


def line_plan(order):
    size = len(order)
    plan, names = {}, {(0, p): (0, 0, 0) for p in range(size)}
    for s in range(1, size):
        edges = {}
        for p in range(size):
            q = order[p][s]
            edges.setdefault(abs(q - p), []).append((p + (1 if q > p else -1), p))
        for distance, group in edges.items():
            split = len({source for source, _ in group}) < len(group)
            for source, p in group:
                name = (distance, s, int(split and source < p))
                names[s, p] = name
                plan.setdefault(name, []).append((source, p))
    held = {
        name: {source: names[order[source].index(order[p][name[1]]), source] for source, p in edges}
        for name, edges in plan.items()
    }
    return plan, held


class Line:
    def __init__(self, own, order):
        self.plan, self.held = line_plan(order)
        self.raw = {(0, 0, 0): own}
        self.sent = 0

    def send(self, *after):
        self.sent += 1
        for name in sorted(self.plan):
            if name[0] == self.sent:
                held = self.held[name]
                some = min(held.values())
                by_plane = [held.get(p, some) for p in range(lax.axis_size("head"))]
                value = tie(pick(by_plane, lambda key: self.raw[key]), *after)
                self.raw[name] = lax.ppermute(value, "head", self.plan[name])

    def close(self, *after):
        names = [name for name in sorted(self.plan) if name[0] == self.sent]
        tied = lax.optimization_barrier(tuple(self.raw[name] for name in names) + after)
        self.raw.update(zip(names, tied))
        return tied[0]

    def slot(self, s):
        return [self.raw[name] for name in sorted(self.raw) if name[1] == s]


def add(a, b):
    rows, width = a.shape
    spec = pl.BlockSpec((rows // 2, width), lambda n: (n, 0))
    return pl.pallas_call(
        add_kernel,
        grid=(2,),
        in_specs=[spec, spec],
        out_specs=spec,
        out_shape=jax.ShapeDtypeStruct(a.shape, BF16),
        compiler_params=PARAMS,
        cost_estimate=LIGHT,
        name="add_rows",
    )(a, b)


class Tree:
    def __init__(self, held, targets, flips):
        self.targets, self.flips = targets, flips
        span = held.shape[1] // len(flips)
        self.now = [held[:, n * span : (n + 1) * span] for n in range(len(flips))]
        self.got, self.turn, self.done = None, 0, [0] * len(flips)

    def send(self, *after):
        count, size = lax.axis_size("tm"), lax.axis_size("head")
        self.got = []
        for n, order in enumerate(self.flips):
            bit = order[self.turn]
            perm = []
            for i in range(count):
                for p in range(size):
                    far = (i // 2) ^ self.targets[p]
                    if far & bit and not far & self.done[n]:
                        perm.append((i * size + p, (i ^ (bit * 2)) * size + p))
            self.got.append(lax.ppermute(tie(self.now[n], *after), ("tm", "head"), perm))
            self.done[n] |= bit

    def take(self, *after):
        got = [tie(x, *after) for x in self.got]
        self.now = [add(x, y) for x, y in zip(self.now, got)]
        self.turn += 1
        self.got = None

    def finished(self):
        return self.turn == len(self.flips[0])


def per_device(query, key, value, grad_out, out_weight, periods, log_decay):
    tok, width = query.shape
    heads = periods.shape[0]
    blocks = tok // BLK
    count, size = lax.axis_size("tm"), lax.axis_size("head")
    group = count // size
    plane = lax.axis_index("head")
    place = lax.axis_index("tm")
    group_bits = [1 << b for b in range(log2_of(size))]
    order = block_order(size)
    assert group == 2

    line = Line(grad_out, order)
    line.send()
    full_weight = lax.all_gather(out_weight, "tm", axis=0, tiled=True)

    factors = pl.pallas_call(
        factors_kernel,
        in_specs=[
            pl.BlockSpec(memory_space=pltpu.SMEM),
            pl.BlockSpec(memory_space=pltpu.VMEM),
            pl.BlockSpec(memory_space=pltpu.VMEM),
        ],
        out_specs=pl.BlockSpec(memory_space=pltpu.VMEM),
        out_shape=jax.ShapeDtypeStruct((heads, 8, tok), F32),
        compiler_params=PARAMS,
            cost_estimate=LIGHT,
        name="factors",
    )((place * tok).astype(jnp.int32)[None], periods[:, None], log_decay)

    half = BLK // 2
    many = math.gcd(heads, 4)
    head_rows = pl.BlockSpec((tok, many * DK), lambda h: (0, h))
    head_factors = pl.BlockSpec((many, 8, tok), lambda h: (h, 0, 0))
    block_states = pl.BlockSpec((many, blocks, DK, DK), lambda h: (h, 0, 0, 0))
    one_state = pl.BlockSpec((many, DK, DK), lambda h: (h, 0, 0))
    weight_rows = BLK + half
    weights_spec = pl.BlockSpec((many, blocks, weight_rows, half), lambda h: (h, 0, 0, 0))
    shape = jax.ShapeDtypeStruct
    states_f32 = shape((heads, blocks, DK, DK), F32)
    states_bf16 = shape((heads, blocks, DK, DK), BF16)
    state_f32 = shape((heads, DK, DK), F32)
    rows_bf16 = shape((tok, width), BF16)

    small = shape((heads, 8, DK), F32)
    fwd_parts, fwd_local, fwd_own, fwd_sent = pl.pallas_call(
        state_kernel,
        grid=(heads // many,),
        in_specs=[head_factors, head_rows, head_rows],
        out_specs=[
            block_states,
            one_state,
            pl.BlockSpec((many, 8, DK), lambda h: (h, 0, 0)),
            pl.BlockSpec((many, DK + 32, DK), lambda h: (h, 0, 0)),
        ],
        out_shape=[states_f32, state_f32, small, shape((heads, DK + 32, DK), BF16)],
        compiler_params=PARAMS,
            cost_estimate=LIGHT,
        name="block_states",
    )(factors, key, value)
    scan = Scan(fwd_local, fwd_own[:, :1], fwd_sent, False)
    scan.send_pair()
    scan.take_pair()
    scan.send_all()
    weights, within = pl.pallas_call(
        within_kernel,
        grid=(heads // many,),
        in_specs=[head_factors, head_rows, head_rows, head_rows],
        out_specs=[weights_spec, head_rows],
        out_shape=[shape((heads, blocks, weight_rows, half), BF16), shape((tok, width), F32)],
        compiler_params=PARAMS,
            cost_estimate=LIGHT,
        name="pair_weights",
    )(tie(factors, scan.pair), query, key, value)
    mark = line.close(within)
    line.send(mark)
    state_in = scan.take_all(mark)
    mixed, states = pl.pallas_call(
        mixed_kernel,
        grid=(heads // many,),
        in_specs=[head_factors, head_rows, head_rows, block_states, one_state],
        out_specs=[head_rows, block_states],
        out_shape=[rows_bf16, states_bf16],
        compiler_params=PARAMS,
            cost_estimate=LIGHT,
        name="mixed_rows",
    )(factors, query, within, fwd_parts, state_in)

    mine = jnp.take(jnp.array(order, jnp.int32), plane, axis=0)

    def targets(s):
        return [order[p][s] for p in range(size)]

    core = (place % 2).astype(jnp.int32)[None]

    sub = grad_out.shape[1] // 4
    whole_mixed = pl.BlockSpec((tok, width), lambda k, i, o: (0, 0))

    def halves_of(arrays, *after):
        block = pl.BlockSpec((tok, sub), lambda k, i, o: (0, 2 * (o[0] ^ (1 - k)) + i))
        out = shape((2 * sub, width), BF16)
        return pl.pallas_call(
            halves_kernel,
            grid_spec=pltpu.PrefetchScalarGridSpec(
                num_scalar_prefetch=1,
                grid=(2, 2),
                in_specs=[block] * len(arrays) + [whole_mixed],
                out_specs=[
                    pl.BlockSpec((sub, width), lambda k, i, o: (jnp.where(k == 0, i, 1), 0)),
                    pl.BlockSpec((sub, width), lambda k, i, o: (jnp.where(k == 0, 0, i), 0)),
                ],
            ),
            out_shape=[out, out],
            compiler_params=PARAMS,
            cost_estimate=LIGHT,
            name="weight_halves",
        )(tie(core, *after), *arrays, mixed)

    def rows_of(slots, held, *after):
        arrays, specs, counts = [], [], []
        for n, s in enumerate(slots):
            mine_of = line.slot(s) if s < size - 1 else []
            counts.append(len(mine_of))
            arrays += mine_of
            specs += [
                pl.BlockSpec((tok, sub), lambda k, i, o, n=n: (0, jnp.where(k == n, i, 3 * (k > n))))
            ] * len(mine_of)
        held = [] if held is None else [held]
        place_of = jnp.stack([mine[s] for s in slots])
        return pl.pallas_call(
            functools.partial(rows_kernel, counts),
            grid_spec=pltpu.PrefetchScalarGridSpec(
                num_scalar_prefetch=1,
                grid=(len(slots), 4),
                in_specs=specs + [whole_mixed] + [pl.BlockSpec(memory_space=pl.ANY)] * len(held),
                out_specs=pl.BlockSpec((sub, width), lambda k, i, o: (o[k] * 4 + i, 0)),
            ),
            out_shape=shape((size * 4 * sub, width), BF16),
            input_output_aliases={len(arrays) + 2: 0} if held else {},
            compiler_params=PARAMS,
            cost_estimate=LIGHT,
            name="weight_rows",
        )(tie(place_of, *after), *arrays, mixed, *held)

    def swap(sent, *after):
        return lax.ppermute(tie(sent, *after), "tm", [(i, i ^ 1) for i in range(count)])

    def joined(kept, got, *after):
        return add(kept, tie(got, *after))

    two = 2 if heads % 2 == 0 else 1
    cover = two * DK
    wide = pl.BlockSpec((tok, cover), lambda n, o: (0, n))
    depth = grad_out.shape[1]

    def accumulate(before, slots, *after):
        inputs = [line.slot(s) for s in slots]
        arrays = [x for y in inputs for x in y]
        held = [] if before is None else [before]
        return pl.pallas_call(
            functools.partial(early_kernel, [len(x) for x in inputs]),
            grid_spec=pltpu.PrefetchScalarGridSpec(
                num_scalar_prefetch=1,
                grid=(width // cover,),
                in_specs=[wide] * len(held)
                + [pl.BlockSpec(x.shape, lambda n, o: (0, 0)) for x in arrays]
                + [pl.BlockSpec((depth, cover), lambda n, o, s=s: (o[s], n)) for s in slots],
                out_specs=wide,
            ),
            out_shape=shape((tok, width), F32),
            compiler_params=PARAMS,
            cost_estimate=LIGHT,
            name="early_product",
        )(tie(mine, *after), *held, *arrays, *[full_weight] * len(slots))

    slots = list(range(min(2, size - 1)))
    products = rows_of(slots, None)
    early = accumulate(None, slots, products)
    for s in range(2, size - 1):
        mark = line.close(early)
        line.send(mark)
        final = [size - 1] if s == size - 2 else []
        products = rows_of([s] + final, products, mark)
        early = accumulate(early, [s], products)
    most = lax.psum_scatter(products, "tm", scatter_dimension=0, tiled=True)
    mark = line.close(early)

    whole = line.slot(size - 1)
    pair_state = pl.BlockSpec((two, DK, DK), lambda n, o: (n, 0, 0))
    e, parts, local, sent = pl.pallas_call(
        functools.partial(grad_kernel, [len(whole)]),
        grid_spec=pltpu.PrefetchScalarGridSpec(
            num_scalar_prefetch=1,
            grid=(width // cover,),
            in_specs=[pl.BlockSpec((two, 8, tok), lambda n, o: (n, 0, 0)), wide, wide]
            + [pl.BlockSpec(x.shape, lambda n, o: (0, 0)) for x in whole]
            + [pl.BlockSpec((depth, cover), lambda n, o: (o[size - 1], n))],
            out_specs=[
                wide,
                pl.BlockSpec((two, blocks, DK, DK), lambda n, o: (n, 0, 0, 0)),
                pair_state,
                pair_state,
            ],
        ),
        out_shape=[rows_bf16, states_f32, state_f32, shape((heads, DK, DK), BF16)],
        compiler_params=PARAMS,
        cost_estimate=LIGHT,
        name="grad_mixed_rows",
    )(mine, factors, query, early, *whole, full_weight)
    back = Scan(local, fwd_own[:, :1], sent, True, scan.known)
    back.send_pair()
    sent, kept = halves_of(whole, e)
    got = swap(sent)
    back.take_pair(kept)
    back.send_all()
    held = joined(kept, got, back.pair)
    last_tree = Tree(held, targets(size - 1), [group_bits[::-1], group_bits])
    last_tree.send()
    own_rows = pl.BlockSpec((BLK, many * DK), lambda h, b: (b, h))
    dq, dk_part, dv_part = pl.pallas_call(
        back_kernel,
        grid=(heads // many, blocks),
        in_specs=[pl.BlockSpec((many, 8, BLK), lambda h, b: (h, 0, b))]
        + [own_rows] * 4
        + [
            pl.BlockSpec((many, 1, weight_rows, half), lambda h, b: (h, b, 0, 0)),
            pl.BlockSpec((many, 1, DK, DK), lambda h, b: (h, b, 0, 0)),
        ],
        out_specs=[own_rows] * 3,
        out_shape=[rows_bf16] * 3,
        compiler_params=PARAMS,
        cost_estimate=LIGHT,
        name="block_gradients",
    )(tie(factors, held), query, key, value, e, weights, states)
    grad_in = back.take_all(dq)
    for _ in group_bits[1:]:
        last_tree.take(grad_in)
        last_tree.send()
    pair_rows = pl.BlockSpec((tok, cover), lambda n: (0, n))
    dk, dv = pl.pallas_call(
        finish_kernel,
        grid=(heads // two,),
        in_specs=[pl.BlockSpec((two, 8, tok), lambda n: (n, 0, 0))]
        + [pair_rows] * 4
        + [
            pl.BlockSpec((two, blocks, DK, DK), lambda n: (n, 0, 0, 0)),
            pl.BlockSpec((two, DK, DK), lambda n: (n, 0, 0)),
        ],
        out_specs=[pair_rows] * 2,
        out_shape=[rows_bf16] * 2,
        compiler_params=PARAMS,
        cost_estimate=LIGHT,
        name="carried_gradients",
    )(factors, key, value, dk_part, dv_part, parts, tie(grad_in, last_tree.now[0]))
    done = [x.astype(F32) + tie(y, dk).astype(F32) for x, y in zip(last_tree.now, last_tree.got)]
    done = jnp.concatenate(done, axis=1)
    grad_weight = most.astype(F32) + jnp.where(mine[size - 1] == place // group, done, 0.0)
    return dq, dk, dv, grad_weight


def solution(mesh):
    both = P("tm", "head")
    return jax.shard_map(
        per_device,
        mesh=mesh,
        in_specs=(both, both, both, both, both, P("head"), P("head", "tm")),
        out_specs=(both, both, both, both),
        check_vma=False,
    )
```

```python
import functools
import math

import jax
import jax.numpy as jnp
from jax import lax
from jax.experimental import pallas as pl
from jax.experimental.pallas import tpu as pltpu
from jax.sharding import PartitionSpec as P

DK = 128
BLK = 512
LOG2E = math.log2(math.e)
FAR = 1e30
F32 = jnp.float32
BF16 = jnp.bfloat16
PARAMS = pltpu.CompilerParams(vmem_limit_bytes=60 * 1024 * 1024)


def dot(a, b, da=1, db=0):
    return lax.dot_general(a, b, (((da,), (db,)), ((), ())), preferred_element_type=F32)


LIGHT = pl.CostEstimate(flops=1, bytes_accessed=1, transcendentals=0)


def factors_kernel(offset, periods, log_decay, out):
    shape = log_decay.shape
    lane = lax.broadcasted_iota(jnp.int32, shape, 1)
    period = jnp.broadcast_to(periods[...], shape)
    update = lax.rem(offset[0] + lane, period) == 0
    cumul = jnp.where(update, period.astype(F32) * log_decay[...], 0.0)
    place = lane % BLK
    step = 1
    while step < BLK:
        cumul = cumul + jnp.where(place >= step, pltpu.roll(cumul, step, 1), 0.0)
        step *= 2
    left = [cumul[:, t : t + BLK] for t in range(0, shape[1], BLK)]
    left = jnp.concatenate([x[:, BLK - 1 : BLK] - x for x in left], axis=1)
    scaled = cumul * LOG2E
    rows = (
        scaled,
        jnp.where(update, jnp.exp(left), 0.0),
        jnp.exp(cumul),
        jnp.where(update, scaled, FAR),
    )
    out[...] = jnp.zeros(out.shape, F32)
    for h in range(shape[0]):
        for r, x in enumerate(rows):
            out[h, r : r + 1, :] = x[h : h + 1, :]


def columns(factors, h=0):
    return jnp.transpose(factors[h])


def pack_decay(sent, h, decay):
    high = decay.astype(BF16)
    low = (decay - high.astype(F32)).astype(BF16)
    sent[h, DK : DK + 16, :] = jnp.broadcast_to(high, (16, DK))
    sent[h, DK + 16 : DK + 32, :] = jnp.broadcast_to(low, (16, DK))


def lanes_of(h):
    return slice(h * DK, (h + 1) * DK)


def state_kernel(factors, k, v, parts, local, own, sent):
    for h in range(parts.shape[0]):
        col, lanes = columns(factors, h), lanes_of(h)
        state = jnp.zeros((DK, DK), F32)
        decay = jnp.ones((1, 1), F32)
        for b in range(parts.shape[1]):
            at, end = b * BLK, (b + 1) * BLK
            scaled = (k[at:end, lanes].astype(F32) * col[at:end, 1:2]).astype(BF16)
            part = dot(scaled, v[at:end, lanes], 0, 0)
            parts[h, b] = part
            fade = col[end - 1 : end, 2:3]
            state = state * fade + part
            decay = decay * fade
        local[h] = state
        own[h] = jnp.broadcast_to(decay, (8, DK))
        sent[h, 0:DK, :] = state.astype(BF16)
        pack_decay(sent, h, jnp.broadcast_to(decay, (1, DK)))


def cut_kernel(rows, out):
    out[...] = rows[...]


def add_kernel(*refs):
    many = len(refs) // 3
    for n in range(many):
        total = refs[n][...].astype(F32) + refs[many + n][...].astype(F32)
        refs[2 * many + n][...] = total.astype(BF16)


def total_block(refs):
    block = refs[0][...]
    for other in refs[1:]:
        block = block + other[...]
    return block


def rows_kernel(counts, order, *refs):
    inputs, mixed, out = refs[: sum(counts)], refs[sum(counts)], refs[-1]
    at = 0
    for n, many in enumerate(counts):
        mine = inputs[at : at + many]
        at += many

        @pl.when(pl.program_id(0) == n)
        def _(mine=mine):
            if mine:
                out[...] = dot(total_block(mine), mixed[...], 0, 0).astype(BF16)
            else:
                out[...] = jnp.zeros(out.shape, BF16)


def masks(col, row, at):
    half = BLK // 2
    out = []
    for start in (0, half):
        spread = jnp.exp2(
            col[at + start : at + BLK, 0:1] - row[:, at + start : at + start + half]
        )
        size = (BLK - start, half)
        causal = lax.broadcasted_iota(jnp.int32, size, 0) >= lax.broadcasted_iota(
            jnp.int32, size, 1
        )
        out.append(jnp.where(causal, spread, 0.0))
    return out


def within_kernel(factors, q, k, v, weights, within):
    half = BLK // 2
    for h in range(weights.shape[0]):
        col, lanes = columns(factors, h), lanes_of(h)
        for b in range(weights.shape[1]):
            at, mid, end = b * BLK, b * BLK + half, (b + 1) * BLK
            first, second = masks(col, factors[h, 3:4, :], at)
            first = (dot(q[at:end, lanes], k[at:mid, lanes], 1, 1) * first).astype(BF16)
            second = (dot(q[mid:end, lanes], k[mid:end, lanes], 1, 1) * second).astype(BF16)
            weights[h, b, 0:BLK, :] = first
            weights[h, b, BLK : BLK + half, :] = second
            part = dot(first, v[at:mid, lanes])
            within[at:mid, lanes] = part[:half]
            within[mid:end, lanes] = part[half:] + dot(second, v[mid:end, lanes])


def mixed_kernel(factors, q, within, parts, start, mixed, states):
    for h in range(parts.shape[0]):
        col, lanes = columns(factors, h), lanes_of(h)
        state = start[h]
        for b in range(parts.shape[1]):
            at, end = b * BLK, (b + 1) * BLK
            small = state.astype(BF16)
            states[h, b] = small
            carried = dot(q[at:end, lanes], small)
            total = within[at:end, lanes] + col[at:end, 2:3] * carried
            mixed[at:end, lanes] = total.astype(BF16)
            state = state * col[end - 1 : end, 2:3] + parts[h, b]


def block_products(counts, rows, blocks):
    total = None
    at = 0
    for n, many in enumerate(counts):
        block = blocks[at][...]
        for other in blocks[at + 1 : at + many]:
            block = block + other[...]
        at += many
        part = dot(block, rows(n))
        total = part if total is None else total + part
    return total


def early_kernel(counts, order, *refs):
    *inputs, out = refs
    shards, inputs = inputs[-len(counts) :], inputs[: -len(counts)]
    before, blocks = (inputs[0], inputs[1:]) if len(inputs) > sum(counts) else (None, inputs)
    total = block_products(counts, lambda n: shards[n][...], blocks)
    out[...] = total if before is None else before[...] + total


def grad_kernel(counts, order, factors, q, early, *refs):
    *blocks, weight, later, e, parts, local, sent = refs
    e[...] = (early[...] + block_products(counts, lambda n: weight[...], blocks)).astype(BF16)
    for h in range(parts.shape[0]):
        col, lanes = columns(factors, h), lanes_of(h)
        scaled = (q[:, lanes].astype(F32) * col[:, 2:3]).astype(BF16)
        part = dot(scaled, e[:, lanes], 0, 0)
        parts[h] = part
        state = later[h] * col[BLK - 1 : BLK, 2:3] + part
        local[h] = state
        sent[h] = state.astype(BF16)


def back_kernel(factors, q, k, v, e, weights, states, *refs):
    dq, dk, dv = refs[-3:]
    half = BLK // 2
    for h in range(weights.shape[0]):
        col, lanes = columns(factors, h), lanes_of(h)
        first, second = masks(col, factors[h, 3:4, :], 0)
        first = (dot(e[:, lanes], v[0:half, lanes], 1, 1) * first).astype(BF16)
        second = (dot(e[half:BLK, lanes], v[half:BLK, lanes], 1, 1) * second).astype(BF16)
        carried = col[:, 2:3] * dot(e[:, lanes], states[h, 0], 1, 1) + dot(first, k[0:half, lanes])
        dq[0:half, lanes] = carried[:half].astype(BF16)
        more = dot(second, k[half:BLK, lanes])
        dq[half:BLK, lanes] = (carried[half:] + more).astype(BF16)
        dk[0:half, lanes] = dot(first, q[:, lanes], 0, 0).astype(BF16)
        dk[half:BLK, lanes] = dot(second, q[half:BLK, lanes], 0, 0).astype(BF16)
        dv[0:half, lanes] = dot(weights[h, 0, 0:BLK, :], e[:, lanes], 0, 0).astype(BF16)
        tail = weights[h, 0, BLK : BLK + half, :]
        dv[half:BLK, lanes] = dot(tail, e[half:BLK, lanes], 0, 0).astype(BF16)


def finish_kernel(factors, k, v, dk_part, dv_part, finish, *refs):
    *parts, dk, dv = refs
    for h in range(finish.shape[0]):
        col, lanes = columns(factors, h), lanes_of(h)
        state = finish[h]
        for b in reversed(range(len(parts))):
            at, end = b * BLK, (b + 1) * BLK
            small = state.astype(BF16)
            factor = col[at:end, 1:2]
            more = factor * dot(v[at:end, lanes], small, 1, 1)
            dk[at:end, lanes] = (dk_part[at:end, lanes].astype(F32) + more).astype(BF16)
            more = factor * dot(k[at:end, lanes], small)
            dv[at:end, lanes] = (dv_part[at:end, lanes].astype(F32) + more).astype(BF16)
            state = state * col[end - 1 : end, 2:3] + parts[b][h]


def log2_of(count):
    bits = count.bit_length() - 1
    assert 1 << bits == count
    return bits


def tie(value, *after):
    return lax.optimization_barrier((value,) + after)[0] if after else value


def call(kernel, *args, out, name, prefetch=0):
    return pl.pallas_call(
        kernel,
        grid_spec=pltpu.PrefetchScalarGridSpec(
            num_scalar_prefetch=prefetch,
            grid=(1,),
            in_specs=[pl.BlockSpec(x.shape, lambda *_, r=x.ndim: (0,) * r) for x in args[prefetch:]],
            out_specs=[pl.BlockSpec(x.shape, lambda *_, r=len(x.shape): (0,) * r) for x in out],
        ),
        out_shape=out,
        compiler_params=PARAMS,
        cost_estimate=LIGHT,
        name=name,
    )(*args)


def with_decay(state, decay):
    high = decay.astype(BF16)
    low = (decay - high.astype(F32)).astype(BF16)
    pair = [jnp.broadcast_to(x, x.shape[:1] + (16, DK)) for x in (high, low)]
    return jnp.concatenate([state.astype(BF16)] + pair, axis=1)


def decay_of(got):
    return got[:, DK : DK + 1, :].astype(F32) + got[:, DK + 16 : DK + 17, :].astype(F32)


class Scan:
    def __init__(self, total, own, sent, reverse, known=None):
        self.total, self.own, self.sent, self.reverse = total, own, sent, reverse
        self.first, self.known = known is None, known or {}

    def permute(self, value, mask):
        count = lax.axis_size("tm")
        return lax.ppermute(value, "tm", [(i, i ^ mask) for i in range(count)])

    def send_pair(self):
        self.got = self.permute(self.sent, 1)

    def take_pair(self, *after):
        got = tie(self.got, *after)
        if self.first:
            self.known[0] = decay_of(got)
        other = self.known[0]
        came = got[:, :DK].astype(F32)
        upper = lax.axis_index("tm") % 2 == 1
        self.takes = upper != self.reverse
        self.near, self.across = came, self.own
        here = jnp.where(self.takes, self.own, 1.0) * came
        self.pair = here + jnp.where(self.takes, 1.0, other) * self.total
        return self.pair

    def send_all(self):
        pairs = lax.axis_size("tm") // 2
        if self.first:
            sent = with_decay(self.pair, self.own * self.known[0])
        else:
            sent = self.pair.astype(BF16)
        self.all = {m: self.permute(sent, 2 * m) for m in range(1, pairs)}

    def take_all(self, *after):
        mine = lax.axis_index("tm") // 2
        got = {m: tie(x, *after) for m, x in self.all.items()}
        if self.first:
            self.known.update({m: decay_of(x) for m, x in got.items()})
        before = (lambda a, b: a > b) if self.reverse else (lambda a, b: a < b)
        state = None
        for m, x in got.items():
            weight = jnp.where(before(mine ^ m, mine), 1.0, 0.0)
            for n in got:
                if n != m:
                    between = before(mine ^ m, mine ^ n) & before(mine ^ n, mine)
                    weight = weight * jnp.where(between, self.known[n], 1.0)
            part = weight * x[:, :DK].astype(F32)
            state = part if state is None else state + part
        other = jnp.where(self.takes, self.known[0], 1.0)
        return other * state + jnp.where(self.takes, self.near, 0.0)


def block_order(size):
    return [sorted(range(size), key=lambda q: (abs(p - q), p ^ q)) for p in range(size)]


def pick(by_plane, make):
    plane = lax.axis_index("head")
    keys = sorted(set(by_plane))
    out = make(keys[0])
    for key in keys[1:]:
        here = functools.reduce(
            jnp.logical_or, [plane == p for p, own in enumerate(by_plane) if own == key]
        )
        out = jnp.where(here, make(key), out)
    return out


def line_plan(order):
    size = len(order)
    plan, names = {}, {(0, p): (0, 0, 0) for p in range(size)}
    for s in range(1, size):
        edges = {}
        for p in range(size):
            q = order[p][s]
            edges.setdefault(abs(q - p), []).append((p + (1 if q > p else -1), p))
        for distance, group in edges.items():
            split = len({source for source, _ in group}) < len(group)
            for source, p in group:
                name = (distance, s, int(split and source < p))
                names[s, p] = name
                plan.setdefault(name, []).append((source, p))
    held = {
        name: {source: names[order[source].index(order[p][name[1]]), source] for source, p in edges}
        for name, edges in plan.items()
    }
    return plan, held


class Line:
    def __init__(self, own, order, spans):
        self.plan, self.held = line_plan(order)
        self.raw = {(0, 0, 0): own}
        self.sent, self.spans = 0, spans
        size = len(order)
        self.cut = {name for name in self.plan if name[0] == size - 1}

    def permute(self, name, value):
        return lax.ppermute(value, "head", self.plan[name])

    def operand(self, name):
        held = self.held[name]
        some = min(held.values())
        by_plane = [held.get(p, some) for p in range(lax.axis_size("head"))]
        return pick(by_plane, lambda key: self.raw[key])

    def send(self, *after):
        self.sent += 1
        for name in sorted(self.plan):
            if name[0] != self.sent:
                continue
            self.raw[name] = self.permute(name, tie(self.operand(name), *after))

    def close(self, *after):
        keys = [k for k in self.raw if (k if len(k) == 3 else k[0])[0] == self.sent]
        tied = lax.optimization_barrier(tuple(self.raw[key] for key in keys) + after)
        self.raw.update(zip(keys, tied))
        return tied[0]

    def send_rows(self, n, ready, *after):
        for name in sorted(self.plan):
            if name[0] == self.sent + 1:
                (held,) = set(self.held[name].values())
                start, end = self.spans[n]
                value = tie(self.raw[held], ready)
                out = jax.ShapeDtypeStruct((end - start, value.shape[1]), BF16)
                part = pl.pallas_call(
                    cut_kernel,
                    grid=(2,),
                    in_specs=[
                        pl.BlockSpec(
                            ((end - start) // 2, value.shape[1]),
                            lambda i, at=start // (end - start): (2 * at + i, 0),
                        )
                    ],
                    out_specs=pl.BlockSpec(((end - start) // 2, value.shape[1]), lambda i: (i, 0)),
                    out_shape=out,
                    compiler_params=PARAMS,
                    cost_estimate=LIGHT,
                    name="cut_rows",
                )(value)
                self.raw[name, n] = self.permute(name, tie(part, *after))

    def newest(self, s):
        return max(name for name in self.plan if name[1] == s)

    def slot(self, s):
        return [self.raw[key] for key in sorted(k for k in self.raw if len(k) == 3) if key[1] == s]

    def last(self, n, *after):
        at = self.spans[n][0] // (self.spans[n][1] - self.spans[n][0])
        whole = [(x, at) for x in self.slot(max(name[1] for name in self.plan))]
        cut = [self.raw[name, n] for name in sorted(self.cut)]
        return whole + [(tie(x, *after), 0) for x in cut]


def add(these, those):
    rows, width = these[0].shape
    spec = pl.BlockSpec((rows // 2, width), lambda n: (n, 0))
    return pl.pallas_call(
        add_kernel,
        grid=(2,),
        in_specs=[spec] * (2 * len(these)),
        out_specs=[spec] * len(these),
        out_shape=[jax.ShapeDtypeStruct(x.shape, BF16) for x in these],
        compiler_params=PARAMS,
        cost_estimate=LIGHT,
        name="add_rows",
    )(*these, *those)


class Tree:
    def __init__(self, held, targets, flips):
        self.targets, self.flips = targets, flips
        span = held.shape[1] // len(flips)
        self.now = [held[:, n * span : (n + 1) * span] for n in range(len(flips))]
        self.got, self.turn, self.done = None, 0, [0] * len(flips)

    def send(self, *after):
        count, size = lax.axis_size("tm"), lax.axis_size("head")
        self.got = []
        for n, order in enumerate(self.flips):
            bit = order[self.turn]
            perm = []
            for i in range(count):
                for p in range(size):
                    far = (i // 2) ^ self.targets[p]
                    if far & bit and not far & self.done[n]:
                        perm.append((i * size + p, (i ^ (bit * 2)) * size + p))
            self.got.append(lax.ppermute(tie(self.now[n], *after), ("tm", "head"), perm))
            self.done[n] |= bit

    def take(self, *after):
        got = [tie(x, *after) for x in self.got]
        self.now = add(self.now, got)
        self.turn += 1
        self.got = None

    def finished(self):
        return self.turn == len(self.flips[0])


def per_device(query, key, value, grad_out, out_weight, periods, log_decay):
    tok, width = query.shape
    heads = periods.shape[0]
    blocks = tok // BLK
    count, size = lax.axis_size("tm"), lax.axis_size("head")
    group = count // size
    plane = lax.axis_index("head")
    place = lax.axis_index("tm")
    group_bits = [1 << b for b in range(log2_of(size))]
    order = block_order(size)
    assert group == 2

    spans = [(b * BLK, (b + 1) * BLK) for b in reversed(range(blocks))]
    line = Line(grad_out, order, spans)
    line.send()
    full_weight = lax.all_gather(out_weight, "tm", axis=0, tiled=True)

    factors = pl.pallas_call(
        factors_kernel,
        in_specs=[
            pl.BlockSpec(memory_space=pltpu.SMEM),
            pl.BlockSpec(memory_space=pltpu.VMEM),
            pl.BlockSpec(memory_space=pltpu.VMEM),
        ],
        out_specs=pl.BlockSpec(memory_space=pltpu.VMEM),
        out_shape=jax.ShapeDtypeStruct((heads, 8, tok), F32),
        compiler_params=PARAMS,
            cost_estimate=LIGHT,
        name="factors",
    )((place * tok).astype(jnp.int32)[None], periods[:, None], log_decay)

    half = BLK // 2
    many = math.gcd(heads, 4)
    head_rows = pl.BlockSpec((tok, many * DK), lambda h: (0, h))
    head_factors = pl.BlockSpec((many, 8, tok), lambda h: (h, 0, 0))
    block_states = pl.BlockSpec((many, blocks, DK, DK), lambda h: (h, 0, 0, 0))
    one_state = pl.BlockSpec((many, DK, DK), lambda h: (h, 0, 0))
    weight_rows = BLK + half
    weights_spec = pl.BlockSpec((many, blocks, weight_rows, half), lambda h: (h, 0, 0, 0))
    shape = jax.ShapeDtypeStruct
    states_f32 = shape((heads, blocks, DK, DK), F32)
    states_bf16 = shape((heads, blocks, DK, DK), BF16)
    state_f32 = shape((heads, DK, DK), F32)
    rows_bf16 = shape((tok, width), BF16)

    small = shape((heads, 8, DK), F32)
    fwd_parts, fwd_local, fwd_own, fwd_sent = pl.pallas_call(
        state_kernel,
        grid=(heads // many,),
        in_specs=[head_factors, head_rows, head_rows],
        out_specs=[
            block_states,
            one_state,
            pl.BlockSpec((many, 8, DK), lambda h: (h, 0, 0)),
            pl.BlockSpec((many, DK + 32, DK), lambda h: (h, 0, 0)),
        ],
        out_shape=[states_f32, state_f32, small, shape((heads, DK + 32, DK), BF16)],
        compiler_params=PARAMS,
            cost_estimate=LIGHT,
        name="block_states",
    )(factors, key, value)
    scan = Scan(fwd_local, fwd_own[:, :1], fwd_sent, False)
    scan.send_pair()
    scan.take_pair()
    scan.send_all()
    weights, within = pl.pallas_call(
        within_kernel,
        grid=(heads // many,),
        in_specs=[head_factors, head_rows, head_rows, head_rows],
        out_specs=[weights_spec, head_rows],
        out_shape=[shape((heads, blocks, weight_rows, half), BF16), shape((tok, width), F32)],
        compiler_params=PARAMS,
            cost_estimate=LIGHT,
        name="pair_weights",
    )(tie(factors, scan.pair), query, key, value)
    mark = line.close(within)
    line.send(mark)
    state_in = scan.take_all(mark)
    mixed, states = pl.pallas_call(
        mixed_kernel,
        grid=(heads // many,),
        in_specs=[head_factors, head_rows, head_rows, block_states, one_state],
        out_specs=[head_rows, block_states],
        out_shape=[rows_bf16, states_bf16],
        compiler_params=PARAMS,
            cost_estimate=LIGHT,
        name="mixed_rows",
    )(factors, query, within, fwd_parts, state_in)

    mine = jnp.take(jnp.array(order, jnp.int32), plane, axis=0)

    def targets(s):
        return [order[p][s] for p in range(size)]

    sub = grad_out.shape[1] // 4
    whole_mixed = pl.BlockSpec((tok, width), lambda k, i, o: (0, 0))

    def rows_of(slots, held, *after):
        arrays, specs, counts = [], [], []
        for n, s in enumerate(slots):
            mine_of = line.slot(s) if s < size - 1 else []
            counts.append(len(mine_of))
            arrays += mine_of
            specs += [
                pl.BlockSpec((tok, sub), lambda k, i, o, n=n: (0, jnp.where(k == n, i, 3 * (k > n))))
            ] * len(mine_of)
        held = [] if held is None else [held]
        place_of = jnp.stack([mine[s] for s in slots])
        return pl.pallas_call(
            functools.partial(rows_kernel, counts),
            grid_spec=pltpu.PrefetchScalarGridSpec(
                num_scalar_prefetch=1,
                grid=(len(slots), 4),
                in_specs=specs + [whole_mixed] + [pl.BlockSpec(memory_space=pl.ANY)] * len(held),
                out_specs=pl.BlockSpec((sub, width), lambda k, i, o: (o[k] * 4 + i, 0)),
            ),
            out_shape=shape((size * 4 * sub, width), BF16),
            input_output_aliases={len(arrays) + 2: 0} if held else {},
            compiler_params=PARAMS,
            cost_estimate=LIGHT,
            name="weight_rows",
        )(tie(place_of, *after), *arrays, mixed, *held)

    def swap(sent, *after):
        return lax.ppermute(tie(sent, *after), "tm", [(i, i ^ 1) for i in range(count)])

    def joined(kept, got, *after):
        return add([kept], [tie(got, *after)])[0]

    two = many
    cover = two * DK
    wide = pl.BlockSpec((tok, cover), lambda n, o: (0, n))
    depth = grad_out.shape[1]

    def accumulate(before, slots, *after):
        inputs = [line.slot(s) for s in slots]
        arrays = [x for y in inputs for x in y]
        held = [] if before is None else [before]
        return pl.pallas_call(
            functools.partial(early_kernel, [len(x) for x in inputs]),
            grid_spec=pltpu.PrefetchScalarGridSpec(
                num_scalar_prefetch=1,
                grid=(width // cover,),
                in_specs=[wide] * len(held)
                + [pl.BlockSpec(x.shape, lambda n, o: (0, 0)) for x in arrays]
                + [pl.BlockSpec((depth, cover), lambda n, o, s=s: (o[s], n)) for s in slots],
                out_specs=wide,
            ),
            out_shape=shape((tok, width), F32),
            compiler_params=PARAMS,
            cost_estimate=LIGHT,
            name="early_product",
        )(tie(mine, *after), *held, *arrays, *[full_weight] * len(slots))

    slots = list(range(min(2, size - 1)))
    def product_of(arrays, *after):
        block = tie(functools.reduce(jnp.add, arrays), *after)
        return dot(block, mixed, 0, 0).astype(BF16)

    products = rows_of(slots + [size - 1], None)
    ready = products
    for s in range(2, size - 1):
        newest = line.raw[line.newest(s)]
        part = product_of([x for x in line.slot(s) if x is not newest], ready)
        mark = line.close(part)
        if s < size - 2:
            line.send(mark)
        else:
            line.send_rows(0, mark, mark)
        product = part + product_of([line.raw[line.newest(s)]], mark)
        ready = products = lax.dynamic_update_slice(products, product, (mine[s] * depth, 0))
    most = lax.psum_scatter(products, "tm", scatter_dimension=0, tiled=True)
    early = accumulate(None, range(size - 1), products)
    later = jnp.zeros((heads, DK, DK), F32)
    pair_state = pl.BlockSpec((two, DK, DK), lambda n, o: (n, 0, 0))
    after, filled = [early], []
    e, parts = {}, {}
    for n, (start, end) in enumerate(spans):
        b = start // BLK
        arrays = line.last(n, *after)
        if n + 1 < blocks:
            line.send_rows(n + 1, early, arrays[-1][0])
        block = functools.reduce(jnp.add, [x[t * BLK : (t + 1) * BLK] for x, t in arrays])
        queue = mine
        if b == 0:
            product = product + dot(block, mixed[start:end], 0, 0)
            product = product.astype(BF16).reshape(2, -1, width)
            first, second = product[0], product[1]
            upper = place % 2 == 1
            got = swap(jnp.where(upper, first, second))
            kept = jnp.where(upper, second, first)
            queue = tie(mine, kept)
        e[b], parts[b], later, sent = pl.pallas_call(
            functools.partial(grad_kernel, [len(arrays)]),
            grid_spec=pltpu.PrefetchScalarGridSpec(
                num_scalar_prefetch=1,
                grid=(width // cover,),
                in_specs=[
                    pl.BlockSpec((two, 8, BLK), lambda n, o, b=b: (n, 0, b)),
                    pl.BlockSpec((BLK, cover), lambda n, o, b=b: (b, n)),
                    pl.BlockSpec((BLK, cover), lambda n, o, b=b: (b, n)),
                ]
                + [pl.BlockSpec((BLK, depth), lambda n, o, at=at: (at, 0)) for _, at in arrays]
                + [pl.BlockSpec((depth, cover), lambda n, o: (o[size - 1], n)), pair_state],
                out_specs=[pl.BlockSpec((BLK, cover), lambda n, o: (0, n))] + [pair_state] * 3,
            ),
            out_shape=[shape((BLK, width), BF16), state_f32, state_f32, shape((heads, DK, DK), BF16)],
            compiler_params=PARAMS,
            cost_estimate=LIGHT,
            name="grad_mixed_rows",
        )(queue, factors, query, early, *[x for x, _ in arrays], full_weight, later)
        if b == 0:
            back = Scan(later, fwd_own[:, :1], sent, True, scan.known)
            back.send_pair()
        order_after = e[b]
        if b:
            part = dot(tie(block, e[b]), mixed[start:end], 0, 0)
            product = part if n == 0 else product + part
            order_after = product
        else:
            held = joined(kept, got, e[b])
            last_tree = Tree(held, targets(size - 1), [group_bits[::-1], group_bits])
            last_tree.send()
            order_after = back.take_pair(held)
            back.send_all()
        own_rows = pl.BlockSpec((BLK, many * DK), lambda h, b=b: (b, h))
        filled = pl.pallas_call(
            back_kernel,
            grid=(heads // many,),
            in_specs=[pl.BlockSpec((many, 8, BLK), lambda h, b=b: (h, 0, b))]
            + [own_rows] * 3
            + [
                pl.BlockSpec((BLK, many * DK), lambda h: (0, h)),
                pl.BlockSpec((many, 1, weight_rows, half), lambda h, b=b: (h, b, 0, 0)),
                pl.BlockSpec((many, 1, DK, DK), lambda h, b=b: (h, b, 0, 0)),
            ]
            + [pl.BlockSpec(memory_space=pl.ANY)] * len(filled),
            out_specs=[own_rows] * 3,
            out_shape=[rows_bf16] * 3,
            input_output_aliases={7 + m: m for m in range(len(filled))},
            compiler_params=PARAMS,
            cost_estimate=LIGHT,
            name="block_gradients",
        )(tie(factors, order_after), query, key, value, e[b], weights, states, *filled)
        after = [filled[0], product]
    dq, dk_part, dv_part = filled
    grad_in = back.take_all(dq)
    for _ in group_bits[1:]:
        last_tree.take(grad_in)
        last_tree.send()
    pair_rows = pl.BlockSpec((tok, cover), lambda n: (0, n))
    dk, dv = pl.pallas_call(
        finish_kernel,
        grid=(heads // two,),
        in_specs=[pl.BlockSpec((two, 8, tok), lambda n: (n, 0, 0))]
        + [pair_rows] * 4
        + [pl.BlockSpec((two, DK, DK), lambda n: (n, 0, 0))] * (1 + blocks),
        out_specs=[pair_rows] * 2,
        out_shape=[rows_bf16] * 2,
        compiler_params=PARAMS,
        cost_estimate=LIGHT,
        name="carried_gradients",
    )(
        factors,
        key,
        value,
        dk_part,
        dv_part,
        tie(grad_in, last_tree.now[0]),
        *[parts[b] for b in range(blocks)],
    )
    done = [x.astype(F32) + tie(y, dk).astype(F32) for x, y in zip(last_tree.now, last_tree.got)]
    done = jnp.concatenate(done, axis=1)
    grad_weight = most.astype(F32) + jnp.where(mine[size - 1] == place // group, done, 0.0)
    return dq, dk, dv, grad_weight


def solution(mesh):
    both = P("tm", "head")
    return jax.shard_map(
        per_device,
        mesh=mesh,
        in_specs=(both, both, both, both, both, P("head"), P("head", "tm")),
        out_specs=(both, both, both, both),
        check_vma=False,
    )
```

```python
import functools
import math

import jax
import jax.numpy as jnp
from jax import lax
from jax.experimental import pallas as pl
from jax.experimental.pallas import tpu as pltpu
from jax.sharding import PartitionSpec as P

DK = 128
BLK = 512
LOG2E = math.log2(math.e)
FAR = 1e30
F32 = jnp.float32
BF16 = jnp.bfloat16
PARAMS = pltpu.CompilerParams(vmem_limit_bytes=60 * 1024 * 1024)


def dot(a, b, da=1, db=0):
    return lax.dot_general(a, b, (((da,), (db,)), ((), ())), preferred_element_type=F32)


LIGHT = pl.CostEstimate(flops=1, bytes_accessed=1, transcendentals=0)


def factors_kernel(offset, periods, log_decay, out):
    shape = log_decay.shape
    lane = lax.broadcasted_iota(jnp.int32, shape, 1)
    period = jnp.broadcast_to(periods[...], shape)
    update = lax.rem(offset[0] + lane, period) == 0
    cumul = jnp.where(update, period.astype(F32) * log_decay[...], 0.0)
    place = lane % BLK
    step = 1
    while step < BLK:
        cumul = cumul + jnp.where(place >= step, pltpu.roll(cumul, step, 1), 0.0)
        step *= 2
    left = [cumul[:, t : t + BLK] for t in range(0, shape[1], BLK)]
    left = jnp.concatenate([x[:, BLK - 1 : BLK] - x for x in left], axis=1)
    scaled = cumul * LOG2E
    rows = (
        scaled,
        jnp.where(update, jnp.exp(left), 0.0),
        jnp.exp(cumul),
        jnp.where(update, scaled, FAR),
    )
    out[...] = jnp.zeros(out.shape, F32)
    for h in range(shape[0]):
        for r, x in enumerate(rows):
            out[h, r : r + 1, :] = x[h : h + 1, :]


def columns(factors, h=0):
    return jnp.transpose(factors[h])


def pack_decay(sent, h, decay):
    high = decay.astype(BF16)
    low = (decay - high.astype(F32)).astype(BF16)
    sent[h, DK : DK + 16, :] = jnp.broadcast_to(high, (16, DK))
    sent[h, DK + 16 : DK + 32, :] = jnp.broadcast_to(low, (16, DK))


def lanes_of(h):
    return slice(h * DK, (h + 1) * DK)


def state_kernel(factors, k, v, parts, local, own, sent):
    for h in range(parts.shape[0]):
        col, lanes = columns(factors, h), lanes_of(h)
        state = jnp.zeros((DK, DK), F32)
        decay = jnp.ones((1, 1), F32)
        for b in range(parts.shape[1]):
            at, end = b * BLK, (b + 1) * BLK
            scaled = (k[at:end, lanes].astype(F32) * col[at:end, 1:2]).astype(BF16)
            part = dot(scaled, v[at:end, lanes], 0, 0)
            parts[h, b] = part
            fade = col[end - 1 : end, 2:3]
            state = state * fade + part
            decay = decay * fade
        local[h] = state
        own[h] = jnp.broadcast_to(decay, (8, DK))
        sent[h, 0:DK, :] = state.astype(BF16)
        pack_decay(sent, h, jnp.broadcast_to(decay, (1, DK)))


def cut_kernel(rows, out):
    out[...] = rows[...]


def add_kernel(cuts, *refs):
    many = len(refs) // (2 + cuts)
    for n in range(many):
        total = refs[n][...].astype(F32) + refs[many + n][...].astype(F32)
        total = total.astype(BF16)
        span = total.shape[1] // cuts
        for m in range(cuts):
            refs[2 * many + n * cuts + m][...] = total[:, m * span : (m + 1) * span]


def total_block(refs):
    block = refs[0][...]
    for other in refs[1:]:
        block = block + other[...]
    return block


def rows_kernel(counts, order, *refs):
    inputs, mixed, out = refs[: sum(counts)], refs[sum(counts)], refs[-1]
    at = 0
    for n, many in enumerate(counts):
        mine = inputs[at : at + many]
        at += many

        @pl.when(pl.program_id(0) == n)
        def _(mine=mine):
            if mine:
                out[...] = dot(total_block(mine), mixed[...], 0, 0).astype(BF16)
            else:
                out[...] = jnp.zeros(out.shape, BF16)


def masks(col, row, at):
    half = BLK // 2
    out = []
    for start in (0, half):
        spread = jnp.exp2(
            col[at + start : at + BLK, 0:1] - row[:, at + start : at + start + half]
        )
        size = (BLK - start, half)
        causal = lax.broadcasted_iota(jnp.int32, size, 0) >= lax.broadcasted_iota(
            jnp.int32, size, 1
        )
        out.append(jnp.where(causal, spread, 0.0))
    return out


def within_kernel(factors, q, k, v, weights, within):
    half = BLK // 2
    for h in range(weights.shape[0]):
        col, lanes = columns(factors, h), lanes_of(h)
        for b in range(weights.shape[1]):
            at, mid, end = b * BLK, b * BLK + half, (b + 1) * BLK
            first, second = masks(col, factors[h, 3:4, :], at)
            first = (dot(q[at:end, lanes], k[at:mid, lanes], 1, 1) * first).astype(BF16)
            second = (dot(q[mid:end, lanes], k[mid:end, lanes], 1, 1) * second).astype(BF16)
            weights[h, b, 0:BLK, :] = first
            weights[h, b, BLK : BLK + half, :] = second
            part = dot(first, v[at:mid, lanes])
            within[at:mid, lanes] = part[:half]
            within[mid:end, lanes] = part[half:] + dot(second, v[mid:end, lanes])


def mixed_kernel(factors, q, within, parts, start, mixed, states):
    for h in range(parts.shape[0]):
        col, lanes = columns(factors, h), lanes_of(h)
        state = start[h]
        for b in range(parts.shape[1]):
            at, end = b * BLK, (b + 1) * BLK
            small = state.astype(BF16)
            states[h, b] = small
            carried = dot(q[at:end, lanes], small)
            total = within[at:end, lanes] + col[at:end, 2:3] * carried
            mixed[at:end, lanes] = total.astype(BF16)
            state = state * col[end - 1 : end, 2:3] + parts[h, b]


def block_products(counts, rows, blocks):
    total = None
    at = 0
    for n, many in enumerate(counts):
        block = blocks[at][...]
        for other in blocks[at + 1 : at + many]:
            block = block + other[...]
        at += many
        part = dot(block, rows(n))
        total = part if total is None else total + part
    return total


def early_kernel(counts, order, *refs):
    *inputs, out = refs
    shards, inputs = inputs[-len(counts) :], inputs[: -len(counts)]
    before, blocks = (inputs[0], inputs[1:]) if len(inputs) > sum(counts) else (None, inputs)
    total = block_products(counts, lambda n: shards[n][...], blocks)
    out[...] = total if before is None else before[...] + total


def grad_kernel(counts, order, factors, q, early, *refs):
    *blocks, weight, later, e, parts, local, sent = refs
    e[...] = (early[...] + block_products(counts, lambda n: weight[...], blocks)).astype(BF16)
    for h in range(parts.shape[0]):
        col, lanes = columns(factors, h), lanes_of(h)
        scaled = (q[:, lanes].astype(F32) * col[:, 2:3]).astype(BF16)
        part = dot(scaled, e[:, lanes], 0, 0)
        parts[h] = part
        state = later[h] * col[BLK - 1 : BLK, 2:3] + part
        local[h] = state
        sent[h] = state.astype(BF16)


def back_kernel(factors, q, k, v, e, weights, states, *refs):
    dq, dk, dv = refs[-3:]
    half = BLK // 2
    for h in range(weights.shape[0]):
        col, lanes = columns(factors, h), lanes_of(h)
        first, second = masks(col, factors[h, 3:4, :], 0)
        first = (dot(e[:, lanes], v[0:half, lanes], 1, 1) * first).astype(BF16)
        second = (dot(e[half:BLK, lanes], v[half:BLK, lanes], 1, 1) * second).astype(BF16)
        carried = col[:, 2:3] * dot(e[:, lanes], states[h, 0], 1, 1) + dot(first, k[0:half, lanes])
        dq[0:half, lanes] = carried[:half].astype(BF16)
        more = dot(second, k[half:BLK, lanes])
        dq[half:BLK, lanes] = (carried[half:] + more).astype(BF16)
        dk[0:half, lanes] = dot(first, q[:, lanes], 0, 0).astype(BF16)
        dk[half:BLK, lanes] = dot(second, q[half:BLK, lanes], 0, 0).astype(BF16)
        dv[0:half, lanes] = dot(weights[h, 0, 0:BLK, :], e[:, lanes], 0, 0).astype(BF16)
        tail = weights[h, 0, BLK : BLK + half, :]
        dv[half:BLK, lanes] = dot(tail, e[half:BLK, lanes], 0, 0).astype(BF16)


def finish_kernel(factors, k, v, dk_part, dv_part, finish, *refs):
    *parts, dk, dv = refs
    for h in range(finish.shape[0]):
        col, lanes = columns(factors, h), lanes_of(h)
        state = finish[h]
        for b in reversed(range(len(parts))):
            at, end = b * BLK, (b + 1) * BLK
            small = state.astype(BF16)
            factor = col[at:end, 1:2]
            more = factor * dot(v[at:end, lanes], small, 1, 1)
            dk[at:end, lanes] = (dk_part[at:end, lanes].astype(F32) + more).astype(BF16)
            more = factor * dot(k[at:end, lanes], small)
            dv[at:end, lanes] = (dv_part[at:end, lanes].astype(F32) + more).astype(BF16)
            state = state * col[end - 1 : end, 2:3] + parts[b][h]


def log2_of(count):
    bits = count.bit_length() - 1
    assert 1 << bits == count
    return bits


def tie(value, *after):
    return lax.optimization_barrier((value,) + after)[0] if after else value


def call(kernel, *args, out, name, prefetch=0):
    return pl.pallas_call(
        kernel,
        grid_spec=pltpu.PrefetchScalarGridSpec(
            num_scalar_prefetch=prefetch,
            grid=(1,),
            in_specs=[pl.BlockSpec(x.shape, lambda *_, r=x.ndim: (0,) * r) for x in args[prefetch:]],
            out_specs=[pl.BlockSpec(x.shape, lambda *_, r=len(x.shape): (0,) * r) for x in out],
        ),
        out_shape=out,
        compiler_params=PARAMS,
        cost_estimate=LIGHT,
        name=name,
    )(*args)


def with_decay(state, decay):
    high = decay.astype(BF16)
    low = (decay - high.astype(F32)).astype(BF16)
    pair = [jnp.broadcast_to(x, x.shape[:1] + (16, DK)) for x in (high, low)]
    return jnp.concatenate([state.astype(BF16)] + pair, axis=1)


def decay_of(got):
    return got[:, DK : DK + 1, :].astype(F32) + got[:, DK + 16 : DK + 17, :].astype(F32)


class Scan:
    def __init__(self, total, own, sent, reverse, known=None):
        self.total, self.own, self.sent, self.reverse = total, own, sent, reverse
        self.first, self.known = known is None, known or {}

    def permute(self, value, mask):
        count = lax.axis_size("tm")
        return lax.ppermute(value, "tm", [(i, i ^ mask) for i in range(count)])

    def send_pair(self):
        self.got = self.permute(self.sent, 1)

    def take_pair(self, *after):
        got = tie(self.got, *after)
        if self.first:
            self.known[0] = decay_of(got)
        other = self.known[0]
        came = got[:, :DK].astype(F32)
        upper = lax.axis_index("tm") % 2 == 1
        self.takes = upper != self.reverse
        self.near, self.across = came, self.own
        here = jnp.where(self.takes, self.own, 1.0) * came
        self.pair = here + jnp.where(self.takes, 1.0, other) * self.total
        return self.pair

    def send_all(self):
        pairs = lax.axis_size("tm") // 2
        if self.first:
            sent = with_decay(self.pair, self.own * self.known[0])
        else:
            sent = self.pair.astype(BF16)
        self.all = {m: self.permute(sent, 2 * m) for m in range(1, pairs)}

    def take_all(self, *after):
        mine = lax.axis_index("tm") // 2
        got = {m: tie(x, *after) for m, x in self.all.items()}
        if self.first:
            self.known.update({m: decay_of(x) for m, x in got.items()})
        before = (lambda a, b: a > b) if self.reverse else (lambda a, b: a < b)
        state = None
        for m, x in got.items():
            weight = jnp.where(before(mine ^ m, mine), 1.0, 0.0)
            for n in got:
                if n != m:
                    between = before(mine ^ m, mine ^ n) & before(mine ^ n, mine)
                    weight = weight * jnp.where(between, self.known[n], 1.0)
            part = weight * x[:, :DK].astype(F32)
            state = part if state is None else state + part
        other = jnp.where(self.takes, self.known[0], 1.0)
        return other * state + jnp.where(self.takes, self.near, 0.0)


def block_order(size):
    return [sorted(range(size), key=lambda q: (abs(p - q), p ^ q)) for p in range(size)]


def pick(by_plane, make):
    plane = lax.axis_index("head")
    keys = sorted(set(by_plane))
    out = make(keys[0])
    for key in keys[1:]:
        here = functools.reduce(
            jnp.logical_or, [plane == p for p, own in enumerate(by_plane) if own == key]
        )
        out = jnp.where(here, make(key), out)
    return out


def line_plan(order):
    size = len(order)
    plan, names = {}, {(0, p): (0, 0, 0) for p in range(size)}
    for s in range(1, size):
        edges = {}
        for p in range(size):
            q = order[p][s]
            edges.setdefault(abs(q - p), []).append((p + (1 if q > p else -1), p))
        for distance, group in edges.items():
            split = len({source for source, _ in group}) < len(group)
            for source, p in group:
                name = (distance, s, int(split and source < p))
                names[s, p] = name
                plan.setdefault(name, []).append((source, p))
    held = {
        name: {source: names[order[source].index(order[p][name[1]]), source] for source, p in edges}
        for name, edges in plan.items()
    }
    return plan, held


class Line:
    def __init__(self, own, order, spans):
        self.plan, self.held = line_plan(order)
        self.raw = {(0, 0, 0): own}
        self.sent, self.spans = 0, spans
        size = len(order)
        self.cut = {name for name in self.plan if name[0] == size - 1}

    def permute(self, name, value):
        return lax.ppermute(value, "head", self.plan[name])

    def operand(self, name):
        held = self.held[name]
        some = min(held.values())
        by_plane = [held.get(p, some) for p in range(lax.axis_size("head"))]
        return pick(by_plane, lambda key: self.raw[key])

    def send(self, *after):
        self.sent += 1
        for name in sorted(self.plan):
            if name[0] != self.sent:
                continue
            self.raw[name] = self.permute(name, tie(self.operand(name), *after))

    def close(self, *after):
        keys = [k for k in self.raw if (k if len(k) == 3 else k[0])[0] == self.sent]
        tied = lax.optimization_barrier(tuple(self.raw[key] for key in keys) + after)
        self.raw.update(zip(keys, tied))
        return tied[0]

    def send_rows(self, n, ready, *after):
        for name in sorted(self.plan):
            if name[0] == self.sent + 1:
                (held,) = set(self.held[name].values())
                start, end = self.spans[n]
                value = tie(self.raw[held], ready)
                out = jax.ShapeDtypeStruct((end - start, value.shape[1]), BF16)
                part = pl.pallas_call(
                    cut_kernel,
                    grid=(2,),
                    in_specs=[
                        pl.BlockSpec(
                            ((end - start) // 2, value.shape[1]),
                            lambda i, at=start // (end - start): (2 * at + i, 0),
                        )
                    ],
                    out_specs=pl.BlockSpec(((end - start) // 2, value.shape[1]), lambda i: (i, 0)),
                    out_shape=out,
                    compiler_params=PARAMS,
                    cost_estimate=LIGHT,
                    name="cut_rows",
                )(value)
                self.raw[name, n] = self.permute(name, tie(part, *after))

    def newest(self, s):
        return max(name for name in self.plan if name[1] == s)

    def slot(self, s):
        return [self.raw[key] for key in sorted(k for k in self.raw if len(k) == 3) if key[1] == s]

    def last(self, n, *after):
        at = self.spans[n][0] // (self.spans[n][1] - self.spans[n][0])
        whole = [(x, at) for x in self.slot(max(name[1] for name in self.plan))]
        cut = [self.raw[name, n] for name in sorted(self.cut)]
        return whole + [(tie(x, *after), 0) for x in cut]


def add(these, those, cuts=1):
    rows, width = these[0].shape
    spec = pl.BlockSpec((rows // 2, width), lambda n: (n, 0))
    part = pl.BlockSpec((rows // 2, width // cuts), lambda n: (n, 0))
    return pl.pallas_call(
        functools.partial(add_kernel, cuts),
        grid=(2,),
        in_specs=[spec] * (2 * len(these)),
        out_specs=[part] * (cuts * len(these)),
        out_shape=[jax.ShapeDtypeStruct((rows, width // cuts), BF16)] * (cuts * len(these)),
        compiler_params=PARAMS,
        cost_estimate=LIGHT,
        name="add_rows",
    )(*these, *those)


class Tree:
    def __init__(self, parts, targets, flips):
        self.targets, self.flips, self.now = targets, flips, list(parts)
        self.got, self.turn, self.done = None, 0, [0] * len(flips)

    def send(self, *after):
        count, size = lax.axis_size("tm"), lax.axis_size("head")
        self.got = []
        for n, order in enumerate(self.flips):
            bit = order[self.turn]
            perm = []
            for i in range(count):
                for p in range(size):
                    far = (i // 2) ^ self.targets[p]
                    if far & bit and not far & self.done[n]:
                        perm.append((i * size + p, (i ^ (bit * 2)) * size + p))
            self.got.append(lax.ppermute(tie(self.now[n], *after), ("tm", "head"), perm))
            self.done[n] |= bit

    def take(self, *after):
        got = [tie(x, *after) for x in self.got]
        self.now = add(self.now, got)
        self.turn += 1
        self.got = None

    def finished(self):
        return self.turn == len(self.flips[0])


def per_device(query, key, value, grad_out, out_weight, periods, log_decay):
    tok, width = query.shape
    heads = periods.shape[0]
    blocks = tok // BLK
    count, size = lax.axis_size("tm"), lax.axis_size("head")
    group = count // size
    plane = lax.axis_index("head")
    place = lax.axis_index("tm")
    group_bits = [1 << b for b in range(log2_of(size))]
    order = block_order(size)
    assert group == 2

    spans = [(b * BLK, (b + 1) * BLK) for b in reversed(range(blocks))]
    line = Line(grad_out, order, spans)
    line.send()
    full_weight = lax.all_gather(out_weight, "tm", axis=0, tiled=True)

    factors = pl.pallas_call(
        factors_kernel,
        in_specs=[
            pl.BlockSpec(memory_space=pltpu.SMEM),
            pl.BlockSpec(memory_space=pltpu.VMEM),
            pl.BlockSpec(memory_space=pltpu.VMEM),
        ],
        out_specs=pl.BlockSpec(memory_space=pltpu.VMEM),
        out_shape=jax.ShapeDtypeStruct((heads, 8, tok), F32),
        compiler_params=PARAMS,
            cost_estimate=LIGHT,
        name="factors",
    )((place * tok).astype(jnp.int32)[None], periods[:, None], log_decay)

    half = BLK // 2
    many = math.gcd(heads, 4)
    head_rows = pl.BlockSpec((tok, many * DK), lambda h: (0, h))
    head_factors = pl.BlockSpec((many, 8, tok), lambda h: (h, 0, 0))
    block_states = pl.BlockSpec((many, blocks, DK, DK), lambda h: (h, 0, 0, 0))
    one_state = pl.BlockSpec((many, DK, DK), lambda h: (h, 0, 0))
    weight_rows = BLK + half
    weights_spec = pl.BlockSpec((many, blocks, weight_rows, half), lambda h: (h, 0, 0, 0))
    shape = jax.ShapeDtypeStruct
    states_f32 = shape((heads, blocks, DK, DK), F32)
    states_bf16 = shape((heads, blocks, DK, DK), BF16)
    state_f32 = shape((heads, DK, DK), F32)
    rows_bf16 = shape((tok, width), BF16)

    small = shape((heads, 8, DK), F32)
    fwd_parts, fwd_local, fwd_own, fwd_sent = pl.pallas_call(
        state_kernel,
        grid=(heads // many,),
        in_specs=[head_factors, head_rows, head_rows],
        out_specs=[
            block_states,
            one_state,
            pl.BlockSpec((many, 8, DK), lambda h: (h, 0, 0)),
            pl.BlockSpec((many, DK + 32, DK), lambda h: (h, 0, 0)),
        ],
        out_shape=[states_f32, state_f32, small, shape((heads, DK + 32, DK), BF16)],
        compiler_params=PARAMS,
            cost_estimate=LIGHT,
        name="block_states",
    )(factors, key, value)
    scan = Scan(fwd_local, fwd_own[:, :1], fwd_sent, False)
    scan.send_pair()
    scan.take_pair()
    scan.send_all()
    weights, within = pl.pallas_call(
        within_kernel,
        grid=(heads // many,),
        in_specs=[head_factors, head_rows, head_rows, head_rows],
        out_specs=[weights_spec, head_rows],
        out_shape=[shape((heads, blocks, weight_rows, half), BF16), shape((tok, width), F32)],
        compiler_params=PARAMS,
            cost_estimate=LIGHT,
        name="pair_weights",
    )(tie(factors, scan.pair), query, key, value)
    mark = line.close(within)
    line.send(mark)
    state_in = scan.take_all(mark)
    mixed, states = pl.pallas_call(
        mixed_kernel,
        grid=(heads // many,),
        in_specs=[head_factors, head_rows, head_rows, block_states, one_state],
        out_specs=[head_rows, block_states],
        out_shape=[rows_bf16, states_bf16],
        compiler_params=PARAMS,
            cost_estimate=LIGHT,
        name="mixed_rows",
    )(factors, query, within, fwd_parts, state_in)

    mine = jnp.take(jnp.array(order, jnp.int32), plane, axis=0)

    def targets(s):
        return [order[p][s] for p in range(size)]

    sub = grad_out.shape[1] // 4
    whole_mixed = pl.BlockSpec((tok, width), lambda k, i, o: (0, 0))

    def rows_of(slots, held, *after):
        arrays, specs, counts = [], [], []
        for n, s in enumerate(slots):
            mine_of = line.slot(s) if s < size - 1 else []
            counts.append(len(mine_of))
            arrays += mine_of
            specs += [
                pl.BlockSpec((tok, sub), lambda k, i, o, n=n: (0, jnp.where(k == n, i, 3 * (k > n))))
            ] * len(mine_of)
        held = [] if held is None else [held]
        place_of = jnp.stack([mine[s] for s in slots])
        return pl.pallas_call(
            functools.partial(rows_kernel, counts),
            grid_spec=pltpu.PrefetchScalarGridSpec(
                num_scalar_prefetch=1,
                grid=(len(slots), 4),
                in_specs=specs + [whole_mixed] + [pl.BlockSpec(memory_space=pl.ANY)] * len(held),
                out_specs=pl.BlockSpec((sub, width), lambda k, i, o: (o[k] * 4 + i, 0)),
            ),
            out_shape=shape((size * 4 * sub, width), BF16),
            input_output_aliases={len(arrays) + 2: 0} if held else {},
            compiler_params=PARAMS,
            cost_estimate=LIGHT,
            name="weight_rows",
        )(tie(place_of, *after), *arrays, mixed, *held)

    def swap(sent, *after):
        return lax.ppermute(tie(sent, *after), "tm", [(i, i ^ 1) for i in range(count)])

    def joined(kept, got, *after):
        return add([kept], [tie(got, *after)], 2)

    two = many
    cover = two * DK
    wide = pl.BlockSpec((tok, cover), lambda n, o: (0, n))
    depth = grad_out.shape[1]

    def accumulate(before, slots, *after):
        inputs = [line.slot(s) for s in slots]
        arrays = [x for y in inputs for x in y]
        held = [] if before is None else [before]
        return pl.pallas_call(
            functools.partial(early_kernel, [len(x) for x in inputs]),
            grid_spec=pltpu.PrefetchScalarGridSpec(
                num_scalar_prefetch=1,
                grid=(width // cover,),
                in_specs=[wide] * len(held)
                + [pl.BlockSpec(x.shape, lambda n, o: (0, 0)) for x in arrays]
                + [pl.BlockSpec((depth, cover), lambda n, o, s=s: (o[s], n)) for s in slots],
                out_specs=wide,
            ),
            out_shape=shape((tok, width), F32),
            compiler_params=PARAMS,
            cost_estimate=LIGHT,
            name="early_product",
        )(tie(mine, *after), *held, *arrays, *[full_weight] * len(slots))

    slots = list(range(min(2, size - 1)))
    def product_of(arrays, *after):
        block = tie(functools.reduce(jnp.add, arrays), *after)
        return dot(block, mixed, 0, 0).astype(BF16)

    products = rows_of(slots + [size - 1], None)
    ready = products
    for s in range(2, size - 1):
        newest = line.raw[line.newest(s)]
        part = product_of([x for x in line.slot(s) if x is not newest], ready)
        mark = line.close(part)
        if s < size - 2:
            line.send(mark)
        else:
            line.send_rows(0, mark, mark)
        product = part + product_of([line.raw[line.newest(s)]], mark)
        ready = products = lax.dynamic_update_slice(products, product, (mine[s] * depth, 0))
    most = lax.psum_scatter(products, "tm", scatter_dimension=0, tiled=True)
    early = accumulate(None, range(size - 1), products)
    later = jnp.zeros((heads, DK, DK), F32)
    pair_state = pl.BlockSpec((two, DK, DK), lambda n, o: (n, 0, 0))
    after, filled = [early], []
    e, parts = {}, {}
    for n, (start, end) in enumerate(spans):
        b = start // BLK
        arrays = line.last(n, *after)
        if n + 1 < blocks:
            line.send_rows(n + 1, early, arrays[-1][0])
        block = functools.reduce(jnp.add, [x[t * BLK : (t + 1) * BLK] for x, t in arrays])
        queue = mine
        if b == 0:
            product = product + dot(block, mixed[start:end], 0, 0)
            product = product.astype(BF16).reshape(2, -1, width)
            first, second = product[0], product[1]
            upper = place % 2 == 1
            got = swap(jnp.where(upper, first, second))
            kept = jnp.where(upper, second, first)
            queue = tie(mine, kept)
        e[b], parts[b], later, sent = pl.pallas_call(
            functools.partial(grad_kernel, [len(arrays)]),
            grid_spec=pltpu.PrefetchScalarGridSpec(
                num_scalar_prefetch=1,
                grid=(width // cover,),
                in_specs=[
                    pl.BlockSpec((two, 8, BLK), lambda n, o, b=b: (n, 0, b)),
                    pl.BlockSpec((BLK, cover), lambda n, o, b=b: (b, n)),
                    pl.BlockSpec((BLK, cover), lambda n, o, b=b: (b, n)),
                ]
                + [pl.BlockSpec((BLK, depth), lambda n, o, at=at: (at, 0)) for _, at in arrays]
                + [pl.BlockSpec((depth, cover), lambda n, o: (o[size - 1], n)), pair_state],
                out_specs=[pl.BlockSpec((BLK, cover), lambda n, o: (0, n))] + [pair_state] * 3,
            ),
            out_shape=[shape((BLK, width), BF16), state_f32, state_f32, shape((heads, DK, DK), BF16)],
            compiler_params=PARAMS,
            cost_estimate=LIGHT,
            name="grad_mixed_rows",
        )(queue, factors, query, early, *[x for x, _ in arrays], full_weight, later)
        if b == 0:
            back = Scan(later, fwd_own[:, :1], sent, True, scan.known)
            back.send_pair()
        order_after = e[b]
        if b:
            part = dot(tie(block, e[b]), mixed[start:end], 0, 0)
            product = part if n == 0 else product + part
            order_after = product
        else:
            held = joined(kept, got, e[b])
            last_tree = Tree(held, targets(size - 1), [group_bits[::-1], group_bits])
            last_tree.send()
            order_after = back.take_pair(held[0])
            back.send_all()
        own_rows = pl.BlockSpec((BLK, many * DK), lambda h, b=b: (b, h))
        filled = pl.pallas_call(
            back_kernel,
            grid=(heads // many,),
            in_specs=[pl.BlockSpec((many, 8, BLK), lambda h, b=b: (h, 0, b))]
            + [own_rows] * 3
            + [
                pl.BlockSpec((BLK, many * DK), lambda h: (0, h)),
                pl.BlockSpec((many, 1, weight_rows, half), lambda h, b=b: (h, b, 0, 0)),
                pl.BlockSpec((many, 1, DK, DK), lambda h, b=b: (h, b, 0, 0)),
            ]
            + [pl.BlockSpec(memory_space=pl.ANY)] * len(filled),
            out_specs=[own_rows] * 3,
            out_shape=[rows_bf16] * 3,
            input_output_aliases={7 + m: m for m in range(len(filled))},
            compiler_params=PARAMS,
            cost_estimate=LIGHT,
            name="block_gradients",
        )(tie(factors, order_after), query, key, value, e[b], weights, states, *filled)
        after = [filled[0], product]
    dq, dk_part, dv_part = filled
    grad_in = back.take_all(dq)
    for _ in group_bits[1:]:
        last_tree.take(dq)
        last_tree.send()
    pair_rows = pl.BlockSpec((tok, cover), lambda n: (0, n))
    dk, dv = pl.pallas_call(
        finish_kernel,
        grid=(heads // two,),
        in_specs=[pl.BlockSpec((two, 8, tok), lambda n: (n, 0, 0))]
        + [pair_rows] * 4
        + [pl.BlockSpec((two, DK, DK), lambda n: (n, 0, 0))] * (1 + blocks),
        out_specs=[pair_rows] * 2,
        out_shape=[rows_bf16] * 2,
        compiler_params=PARAMS,
        cost_estimate=LIGHT,
        name="carried_gradients",
    )(
        factors,
        key,
        value,
        dk_part,
        dv_part,
        grad_in,
        *[parts[b] for b in range(blocks)],
    )
    done = [x.astype(F32) + tie(y, dk).astype(F32) for x, y in zip(last_tree.now, last_tree.got)]
    done = jnp.concatenate(done, axis=1)
    grad_weight = most.astype(F32) + jnp.where(mine[size - 1] == place // group, done, 0.0)
    return dq, dk, dv, grad_weight


def solution(mesh):
    both = P("tm", "head")
    return jax.shard_map(
        per_device,
        mesh=mesh,
        in_specs=(both, both, both, both, both, P("head"), P("head", "tm")),
        out_specs=(both, both, both, both),
        check_vma=False,
    )
```

```python
import functools
import math

import jax
import jax.numpy as jnp
from jax import lax
from jax.experimental import pallas as pl
from jax.experimental.pallas import tpu as pltpu
from jax.sharding import PartitionSpec as P

DK = 128
BLK = 512
LOG2E = math.log2(math.e)
FAR = 1e30
F32 = jnp.float32
BF16 = jnp.bfloat16
PARAMS = pltpu.CompilerParams(vmem_limit_bytes=60 * 1024 * 1024)


def dot(a, b, da=1, db=0):
    return lax.dot_general(a, b, (((da,), (db,)), ((), ())), preferred_element_type=F32)


LIGHT = pl.CostEstimate(flops=1, bytes_accessed=1, transcendentals=0)


def factors_kernel(offset, periods, log_decay, out):
    shape = log_decay.shape
    lane = lax.broadcasted_iota(jnp.int32, shape, 1)
    period = jnp.broadcast_to(periods[...], shape)
    update = lax.rem(offset[0] + lane, period) == 0
    cumul = jnp.where(update, period.astype(F32) * log_decay[...], 0.0)
    place = lane % BLK
    step = 1
    while step < BLK:
        cumul = cumul + jnp.where(place >= step, pltpu.roll(cumul, step, 1), 0.0)
        step *= 2
    left = [cumul[:, t : t + BLK] for t in range(0, shape[1], BLK)]
    left = jnp.concatenate([x[:, BLK - 1 : BLK] - x for x in left], axis=1)
    scaled = cumul * LOG2E
    rows = (
        scaled,
        jnp.where(update, jnp.exp(left), 0.0),
        jnp.exp(cumul),
        jnp.where(update, scaled, FAR),
    )
    out[...] = jnp.zeros(out.shape, F32)
    for h in range(shape[0]):
        for r, x in enumerate(rows):
            out[h, r : r + 1, :] = x[h : h + 1, :]


def columns(factors, h=0):
    return jnp.transpose(factors[h])


def pack_decay(sent, h, decay):
    high = decay.astype(BF16)
    low = (decay - high.astype(F32)).astype(BF16)
    sent[h, DK : DK + 16, :] = jnp.broadcast_to(high, (16, DK))
    sent[h, DK + 16 : DK + 32, :] = jnp.broadcast_to(low, (16, DK))


def lanes_of(h):
    return slice(h * DK, (h + 1) * DK)


def state_kernel(factors, k, v, parts, local, own, sent):
    for h in range(parts.shape[0]):
        col, lanes = columns(factors, h), lanes_of(h)
        state = jnp.zeros((DK, DK), F32)
        decay = jnp.ones((1, 1), F32)
        for b in range(parts.shape[1]):
            at, end = b * BLK, (b + 1) * BLK
            scaled = (k[at:end, lanes].astype(F32) * col[at:end, 1:2]).astype(BF16)
            part = dot(scaled, v[at:end, lanes], 0, 0)
            parts[h, b] = part
            fade = col[end - 1 : end, 2:3]
            state = state * fade + part
            decay = decay * fade
        local[h] = state
        own[h] = jnp.broadcast_to(decay, (8, DK))
        sent[h, 0:DK, :] = state.astype(BF16)
        pack_decay(sent, h, jnp.broadcast_to(decay, (1, DK)))


def cut_kernel(rows, out):
    out[...] = rows[...]


def add_kernel(cuts, *refs):
    many = len(refs) // (2 + cuts)
    for n in range(many):
        total = refs[n][...].astype(F32) + refs[many + n][...].astype(F32)
        total = total.astype(BF16)
        span = total.shape[1] // cuts
        for m in range(cuts):
            refs[2 * many + n * cuts + m][...] = total[:, m * span : (m + 1) * span]


def total_block(refs):
    block = refs[0][...]
    for other in refs[1:]:
        block = block + other[...]
    return block


def rows_kernel(counts, order, *refs):
    inputs, mixed, out = refs[: sum(counts)], refs[sum(counts)], refs[-1]
    at = 0
    for n, many in enumerate(counts):
        mine = inputs[at : at + many]
        at += many

        @pl.when(pl.program_id(0) == n)
        def _(mine=mine):
            if mine:
                out[...] = dot(total_block(mine), mixed[...], 0, 0).astype(BF16)
            else:
                out[...] = jnp.zeros(out.shape, BF16)


def masks(col, row, at):
    half = BLK // 2
    out = []
    for start in (0, half):
        spread = jnp.exp2(
            col[at + start : at + BLK, 0:1] - row[:, at + start : at + start + half]
        )
        size = (BLK - start, half)
        causal = lax.broadcasted_iota(jnp.int32, size, 0) >= lax.broadcasted_iota(
            jnp.int32, size, 1
        )
        out.append(jnp.where(causal, spread, 0.0))
    return out


def within_kernel(factors, q, k, v, weights, within):
    half = BLK // 2
    for h in range(weights.shape[0]):
        col, lanes = columns(factors, h), lanes_of(h)
        for b in range(weights.shape[1]):
            at, mid, end = b * BLK, b * BLK + half, (b + 1) * BLK
            first, second = masks(col, factors[h, 3:4, :], at)
            first = (dot(q[at:end, lanes], k[at:mid, lanes], 1, 1) * first).astype(BF16)
            second = (dot(q[mid:end, lanes], k[mid:end, lanes], 1, 1) * second).astype(BF16)
            weights[h, b, 0:BLK, :] = first
            weights[h, b, BLK : BLK + half, :] = second
            part = dot(first, v[at:mid, lanes])
            within[at:mid, lanes] = part[:half]
            within[mid:end, lanes] = part[half:] + dot(second, v[mid:end, lanes])


def mixed_kernel(factors, q, within, parts, start, mixed, states):
    for h in range(parts.shape[0]):
        col, lanes = columns(factors, h), lanes_of(h)
        state = start[h]
        for b in range(parts.shape[1]):
            at, end = b * BLK, (b + 1) * BLK
            small = state.astype(BF16)
            states[h, b] = small
            carried = dot(q[at:end, lanes], small)
            total = within[at:end, lanes] + col[at:end, 2:3] * carried
            mixed[at:end, lanes] = total.astype(BF16)
            state = state * col[end - 1 : end, 2:3] + parts[h, b]


def block_products(counts, rows, blocks):
    total = None
    at = 0
    for n, many in enumerate(counts):
        block = blocks[at][...]
        for other in blocks[at + 1 : at + many]:
            block = block + other[...]
        at += many
        part = dot(block, rows(n))
        total = part if total is None else total + part
    return total


def early_kernel(counts, order, *refs):
    *inputs, out = refs
    shards, inputs = inputs[-len(counts) :], inputs[: -len(counts)]
    before, blocks = (inputs[0], inputs[1:]) if len(inputs) > sum(counts) else (None, inputs)
    total = block_products(counts, lambda n: shards[n][...], blocks)
    out[...] = total if before is None else before[...] + total


def grad_kernel(counts, order, factors, q, early, *refs):
    *blocks, weight, later, e, parts, local, sent = refs
    e[...] = (early[...] + block_products(counts, lambda n: weight[...], blocks)).astype(BF16)
    for h in range(parts.shape[0]):
        col, lanes = columns(factors, h), lanes_of(h)
        scaled = (q[:, lanes].astype(F32) * col[:, 2:3]).astype(BF16)
        part = dot(scaled, e[:, lanes], 0, 0)
        parts[h] = part
        state = later[h] * col[BLK - 1 : BLK, 2:3] + part
        local[h] = state
        sent[h] = state.astype(BF16)


def back_kernel(factors, q, k, v, e, weights, states, *refs):
    dq, dk, dv = refs[-3:]
    half = BLK // 2
    for h in range(weights.shape[0]):
        col, lanes = columns(factors, h), lanes_of(h)
        first, second = masks(col, factors[h, 3:4, :], 0)
        first = (dot(e[:, lanes], v[0:half, lanes], 1, 1) * first).astype(BF16)
        second = (dot(e[half:BLK, lanes], v[half:BLK, lanes], 1, 1) * second).astype(BF16)
        carried = col[:, 2:3] * dot(e[:, lanes], states[h, 0], 1, 1) + dot(first, k[0:half, lanes])
        dq[0:half, lanes] = carried[:half].astype(BF16)
        more = dot(second, k[half:BLK, lanes])
        dq[half:BLK, lanes] = (carried[half:] + more).astype(BF16)
        dk[0:half, lanes] = dot(first, q[:, lanes], 0, 0).astype(BF16)
        dk[half:BLK, lanes] = dot(second, q[half:BLK, lanes], 0, 0).astype(BF16)
        dv[0:half, lanes] = dot(weights[h, 0, 0:BLK, :], e[:, lanes], 0, 0).astype(BF16)
        tail = weights[h, 0, BLK : BLK + half, :]
        dv[half:BLK, lanes] = dot(tail, e[half:BLK, lanes], 0, 0).astype(BF16)


def finish_kernel(factors, k, v, dk_part, dv_part, finish, *refs):
    *parts, dk, dv = refs
    for h in range(finish.shape[0]):
        col, lanes = columns(factors, h), lanes_of(h)
        state = finish[h]
        for b in reversed(range(len(parts))):
            at, end = b * BLK, (b + 1) * BLK
            small = state.astype(BF16)
            factor = col[at:end, 1:2]
            more = factor * dot(v[at:end, lanes], small, 1, 1)
            dk[at:end, lanes] = (dk_part[at:end, lanes].astype(F32) + more).astype(BF16)
            more = factor * dot(k[at:end, lanes], small)
            dv[at:end, lanes] = (dv_part[at:end, lanes].astype(F32) + more).astype(BF16)
            state = state * col[end - 1 : end, 2:3] + parts[b][h]


def log2_of(count):
    bits = count.bit_length() - 1
    assert 1 << bits == count
    return bits


def tie(value, *after):
    return lax.optimization_barrier((value,) + after)[0] if after else value


def call(kernel, *args, out, name, prefetch=0):
    return pl.pallas_call(
        kernel,
        grid_spec=pltpu.PrefetchScalarGridSpec(
            num_scalar_prefetch=prefetch,
            grid=(1,),
            in_specs=[pl.BlockSpec(x.shape, lambda *_, r=x.ndim: (0,) * r) for x in args[prefetch:]],
            out_specs=[pl.BlockSpec(x.shape, lambda *_, r=len(x.shape): (0,) * r) for x in out],
        ),
        out_shape=out,
        compiler_params=PARAMS,
        cost_estimate=LIGHT,
        name=name,
    )(*args)


def with_decay(state, decay):
    high = decay.astype(BF16)
    low = (decay - high.astype(F32)).astype(BF16)
    pair = [jnp.broadcast_to(x, x.shape[:1] + (16, DK)) for x in (high, low)]
    return jnp.concatenate([state.astype(BF16)] + pair, axis=1)


def decay_of(got):
    return got[:, DK : DK + 1, :].astype(F32) + got[:, DK + 16 : DK + 17, :].astype(F32)


class Scan:
    def __init__(self, total, own, sent, reverse, known=None):
        self.total, self.own, self.sent, self.reverse = total, own, sent, reverse
        self.first, self.known = known is None, known or {}

    def permute(self, value, mask):
        count = lax.axis_size("tm")
        return lax.ppermute(value, "tm", [(i, i ^ mask) for i in range(count)])

    def send_pair(self):
        self.got = self.permute(self.sent, 1)

    def take_pair(self, *after):
        got = tie(self.got, *after)
        if self.first:
            self.known[0] = decay_of(got)
        other = self.known[0]
        came = got[:, :DK].astype(F32)
        upper = lax.axis_index("tm") % 2 == 1
        self.takes = upper != self.reverse
        self.near, self.across = came, self.own
        here = jnp.where(self.takes, self.own, 1.0) * came
        self.pair = here + jnp.where(self.takes, 1.0, other) * self.total
        return self.pair

    def send_all(self):
        pairs = lax.axis_size("tm") // 2
        if self.first:
            sent = with_decay(self.pair, self.own * self.known[0])
        else:
            sent = self.pair.astype(BF16)
        self.all = {m: self.permute(sent, 2 * m) for m in range(1, pairs)}

    def take_all(self, *after):
        mine = lax.axis_index("tm") // 2
        got = {m: tie(x, *after) for m, x in self.all.items()}
        if self.first:
            self.known.update({m: decay_of(x) for m, x in got.items()})
        before = (lambda a, b: a > b) if self.reverse else (lambda a, b: a < b)
        state = None
        for m, x in got.items():
            weight = jnp.where(before(mine ^ m, mine), 1.0, 0.0)
            for n in got:
                if n != m:
                    between = before(mine ^ m, mine ^ n) & before(mine ^ n, mine)
                    weight = weight * jnp.where(between, self.known[n], 1.0)
            part = weight * x[:, :DK].astype(F32)
            state = part if state is None else state + part
        other = jnp.where(self.takes, self.known[0], 1.0)
        return other * state + jnp.where(self.takes, self.near, 0.0)


def block_order(size):
    return [sorted(range(size), key=lambda q: (abs(p - q), p ^ q)) for p in range(size)]


def pick(by_plane, make):
    plane = lax.axis_index("head")
    keys = sorted(set(by_plane))
    out = make(keys[0])
    for key in keys[1:]:
        here = functools.reduce(
            jnp.logical_or, [plane == p for p, own in enumerate(by_plane) if own == key]
        )
        out = jnp.where(here, make(key), out)
    return out


def line_plan(order):
    size = len(order)
    plan, names = {}, {(0, p): (0, 0, 0) for p in range(size)}
    for s in range(1, size):
        edges = {}
        for p in range(size):
            q = order[p][s]
            edges.setdefault(abs(q - p), []).append((p + (1 if q > p else -1), p))
        for distance, group in edges.items():
            split = len({source for source, _ in group}) < len(group)
            for source, p in group:
                name = (distance, s, int(split and source < p))
                names[s, p] = name
                plan.setdefault(name, []).append((source, p))
    held = {
        name: {source: names[order[source].index(order[p][name[1]]), source] for source, p in edges}
        for name, edges in plan.items()
    }
    return plan, held


class Line:
    def __init__(self, own, order, spans):
        self.plan, self.held = line_plan(order)
        self.raw = {(0, 0, 0): own}
        self.sent, self.spans = 0, spans
        size = len(order)
        self.cut = {name for name in self.plan if name[0] == size - 1}

    def permute(self, name, value):
        return lax.ppermute(value, "head", self.plan[name])

    def operand(self, name):
        held = self.held[name]
        some = min(held.values())
        by_plane = [held.get(p, some) for p in range(lax.axis_size("head"))]
        return pick(by_plane, lambda key: self.raw[key])

    def send(self, *after):
        self.sent += 1
        for name in sorted(self.plan):
            if name[0] != self.sent:
                continue
            self.raw[name] = self.permute(name, tie(self.operand(name), *after))

    def close(self, *after):
        keys = [k for k in self.raw if (k if len(k) == 3 else k[0])[0] == self.sent]
        tied = lax.optimization_barrier(tuple(self.raw[key] for key in keys) + after)
        self.raw.update(zip(keys, tied))
        return tied[0]

    def send_rows(self, n, ready, *after):
        for name in sorted(self.plan):
            if name[0] == self.sent + 1:
                (held,) = set(self.held[name].values())
                start, end = self.spans[n]
                value = tie(self.raw[held], ready)
                out = jax.ShapeDtypeStruct((end - start, value.shape[1]), BF16)
                part = pl.pallas_call(
                    cut_kernel,
                    grid=(2,),
                    in_specs=[
                        pl.BlockSpec(
                            ((end - start) // 2, value.shape[1]),
                            lambda i, at=start // (end - start): (2 * at + i, 0),
                        )
                    ],
                    out_specs=pl.BlockSpec(((end - start) // 2, value.shape[1]), lambda i: (i, 0)),
                    out_shape=out,
                    compiler_params=PARAMS,
                    cost_estimate=LIGHT,
                    name="cut_rows",
                )(value)
                self.raw[name, n] = self.permute(name, tie(part, *after))

    def newest(self, s):
        return max(name for name in self.plan if name[1] == s)

    def slot(self, s):
        return [self.raw[key] for key in sorted(k for k in self.raw if len(k) == 3) if key[1] == s]

    def last(self, n, *after):
        at = self.spans[n][0] // (self.spans[n][1] - self.spans[n][0])
        whole = [(x, at) for x in self.slot(max(name[1] for name in self.plan))]
        cut = [self.raw[name, n] for name in sorted(self.cut)]
        return whole + [(tie(x, *after), 0) for x in cut]


def add(these, those, cuts=1):
    rows, width = these[0].shape
    spec = pl.BlockSpec((rows // 2, width), lambda n: (n, 0))
    part = pl.BlockSpec((rows // 2, width // cuts), lambda n: (n, 0))
    return pl.pallas_call(
        functools.partial(add_kernel, cuts),
        grid=(2,),
        in_specs=[spec] * (2 * len(these)),
        out_specs=[part] * (cuts * len(these)),
        out_shape=[jax.ShapeDtypeStruct((rows, width // cuts), BF16)] * (cuts * len(these)),
        compiler_params=PARAMS,
        cost_estimate=LIGHT,
        name="add_rows",
    )(*these, *those)


class Tree:
    def __init__(self, parts, targets, flips):
        self.targets, self.flips, self.now = targets, flips, list(parts)
        self.got, self.turn, self.done = None, 0, [0] * len(flips)

    def send(self, *after):
        count, size = lax.axis_size("tm"), lax.axis_size("head")
        self.got = []
        for n, order in enumerate(self.flips):
            bit = order[self.turn]
            perm = []
            for i in range(count):
                for p in range(size):
                    far = (i // 2) ^ self.targets[p]
                    if far & bit and not far & self.done[n]:
                        perm.append((i * size + p, (i ^ (bit * 2)) * size + p))
            self.got.append(lax.ppermute(tie(self.now[n], *after), ("tm", "head"), perm))
            self.done[n] |= bit

    def take(self, *after):
        got = [tie(x, *after) for x in self.got]
        self.now = add(self.now, got)
        self.turn += 1
        self.got = None

    def finished(self):
        return self.turn == len(self.flips[0])


def per_device(query, key, value, grad_out, out_weight, periods, log_decay):
    tok, width = query.shape
    heads = periods.shape[0]
    blocks = tok // BLK
    count, size = lax.axis_size("tm"), lax.axis_size("head")
    group = count // size
    plane = lax.axis_index("head")
    place = lax.axis_index("tm")
    group_bits = [1 << b for b in range(log2_of(size))]
    order = block_order(size)
    assert group == 2

    spans = [(b * BLK, (b + 1) * BLK) for b in reversed(range(blocks))]
    line = Line(grad_out, order, spans)
    line.send()
    full_weight = lax.all_gather(out_weight, "tm", axis=0, tiled=True)

    factors = pl.pallas_call(
        factors_kernel,
        in_specs=[
            pl.BlockSpec(memory_space=pltpu.SMEM),
            pl.BlockSpec(memory_space=pltpu.VMEM),
            pl.BlockSpec(memory_space=pltpu.VMEM),
        ],
        out_specs=pl.BlockSpec(memory_space=pltpu.VMEM),
        out_shape=jax.ShapeDtypeStruct((heads, 8, tok), F32),
        compiler_params=PARAMS,
            cost_estimate=LIGHT,
        name="factors",
    )((place * tok).astype(jnp.int32)[None], periods[:, None], log_decay)

    half = BLK // 2
    many = math.gcd(heads, 4)
    head_rows = pl.BlockSpec((tok, many * DK), lambda h: (0, h))
    head_factors = pl.BlockSpec((many, 8, tok), lambda h: (h, 0, 0))
    block_states = pl.BlockSpec((many, blocks, DK, DK), lambda h: (h, 0, 0, 0))
    one_state = pl.BlockSpec((many, DK, DK), lambda h: (h, 0, 0))
    weight_rows = BLK + half
    weights_spec = pl.BlockSpec((many, blocks, weight_rows, half), lambda h: (h, 0, 0, 0))
    shape = jax.ShapeDtypeStruct
    states_f32 = shape((heads, blocks, DK, DK), F32)
    states_bf16 = shape((heads, blocks, DK, DK), BF16)
    state_f32 = shape((heads, DK, DK), F32)
    rows_bf16 = shape((tok, width), BF16)

    small = shape((heads, 8, DK), F32)
    fwd_parts, fwd_local, fwd_own, fwd_sent = pl.pallas_call(
        state_kernel,
        grid=(heads // many,),
        in_specs=[head_factors, head_rows, head_rows],
        out_specs=[
            block_states,
            one_state,
            pl.BlockSpec((many, 8, DK), lambda h: (h, 0, 0)),
            pl.BlockSpec((many, DK + 32, DK), lambda h: (h, 0, 0)),
        ],
        out_shape=[states_f32, state_f32, small, shape((heads, DK + 32, DK), BF16)],
        compiler_params=PARAMS,
            cost_estimate=LIGHT,
        name="block_states",
    )(factors, key, value)
    scan = Scan(fwd_local, fwd_own[:, :1], fwd_sent, False)
    scan.send_pair()
    scan.take_pair()
    scan.send_all()
    weights, within = pl.pallas_call(
        within_kernel,
        grid=(heads // many,),
        in_specs=[head_factors, head_rows, head_rows, head_rows],
        out_specs=[weights_spec, head_rows],
        out_shape=[shape((heads, blocks, weight_rows, half), BF16), shape((tok, width), F32)],
        compiler_params=PARAMS,
            cost_estimate=LIGHT,
        name="pair_weights",
    )(tie(factors, scan.pair), query, key, value)
    mark = line.close(within)
    line.send(mark)
    state_in = scan.take_all(mark)
    mixed, states = pl.pallas_call(
        mixed_kernel,
        grid=(heads // many,),
        in_specs=[head_factors, head_rows, head_rows, block_states, one_state],
        out_specs=[head_rows, block_states],
        out_shape=[rows_bf16, states_bf16],
        compiler_params=PARAMS,
            cost_estimate=LIGHT,
        name="mixed_rows",
    )(factors, query, within, fwd_parts, state_in)

    mine = jnp.take(jnp.array(order, jnp.int32), plane, axis=0)

    def targets(s):
        return [order[p][s] for p in range(size)]

    sub = grad_out.shape[1] // 4
    whole_mixed = pl.BlockSpec((tok, width), lambda k, i, o: (0, 0))

    def rows_of(slots, held, *after):
        arrays, specs, counts = [], [], []
        for n, s in enumerate(slots):
            mine_of = line.slot(s) if s < size - 1 else []
            counts.append(len(mine_of))
            arrays += mine_of
            specs += [
                pl.BlockSpec((tok, sub), lambda k, i, o, n=n: (0, jnp.where(k == n, i, 3 * (k > n))))
            ] * len(mine_of)
        held = [] if held is None else [held]
        place_of = jnp.stack([mine[s] for s in slots])
        return pl.pallas_call(
            functools.partial(rows_kernel, counts),
            grid_spec=pltpu.PrefetchScalarGridSpec(
                num_scalar_prefetch=1,
                grid=(len(slots), 4),
                in_specs=specs + [whole_mixed] + [pl.BlockSpec(memory_space=pl.ANY)] * len(held),
                out_specs=pl.BlockSpec((sub, width), lambda k, i, o: (o[k] * 4 + i, 0)),
            ),
            out_shape=shape((size * 4 * sub, width), BF16),
            input_output_aliases={len(arrays) + 2: 0} if held else {},
            compiler_params=PARAMS,
            cost_estimate=LIGHT,
            name="weight_rows",
        )(tie(place_of, *after), *arrays, mixed, *held)

    def swap(sent, *after):
        return lax.ppermute(tie(sent, *after), "tm", [(i, i ^ 1) for i in range(count)])

    def joined(kept, got, *after):
        return add([kept], [tie(got, *after)], 2)

    two = many
    cover = two * DK
    wide = pl.BlockSpec((tok, cover), lambda n, o: (0, n))
    depth = grad_out.shape[1]

    def accumulate(before, slots, *after):
        inputs = [line.slot(s) for s in slots]
        arrays = [x for y in inputs for x in y]
        held = [] if before is None else [before]
        return pl.pallas_call(
            functools.partial(early_kernel, [len(x) for x in inputs]),
            grid_spec=pltpu.PrefetchScalarGridSpec(
                num_scalar_prefetch=1,
                grid=(width // cover,),
                in_specs=[wide] * len(held)
                + [pl.BlockSpec(x.shape, lambda n, o: (0, 0)) for x in arrays]
                + [pl.BlockSpec((depth, cover), lambda n, o, s=s: (o[s], n)) for s in slots],
                out_specs=wide,
            ),
            out_shape=shape((tok, width), F32),
            compiler_params=PARAMS,
            cost_estimate=LIGHT,
            name="early_product",
        )(tie(mine, *after), *held, *arrays, *[full_weight] * len(slots))

    slots = list(range(min(2, size - 1)))
    def product_of(arrays, *after):
        block = tie(functools.reduce(jnp.add, arrays), *after)
        return dot(block, mixed, 0, 0).astype(BF16)

    products = rows_of(slots + [size - 1], None)
    ready = products
    for s in range(2, size - 1):
        newest = line.raw[line.newest(s)]
        part = product_of([x for x in line.slot(s) if x is not newest], ready)
        mark = line.close(part)
        if s < size - 2:
            line.send(mark)
        else:
            line.send_rows(0, mark, mark)
        product = part + product_of([line.raw[line.newest(s)]], mark)
        ready = products = lax.dynamic_update_slice(products, product, (mine[s] * depth, 0))
    most = lax.psum_scatter(products, "tm", scatter_dimension=0, tiled=True)
    early = accumulate(None, range(size - 1), products)
    later = jnp.zeros((heads, DK, DK), F32)
    pair_state = pl.BlockSpec((two, DK, DK), lambda n, o: (n, 0, 0))
    after, filled = [early], []
    e, parts = {}, {}
    for n, (start, end) in enumerate(spans):
        b = start // BLK
        arrays = line.last(n, *after)
        if n + 1 < blocks:
            line.send_rows(n + 1, early, arrays[-1][0])
        block = functools.reduce(jnp.add, [x[t * BLK : (t + 1) * BLK] for x, t in arrays])
        queue = mine
        if b == 0:
            product = product + dot(block, mixed[start:end], 0, 0)
            product = product.astype(BF16).reshape(2, -1, width)
            first, second = product[0], product[1]
            upper = place % 2 == 1
            got = swap(jnp.where(upper, first, second))
            kept = jnp.where(upper, second, first)
            queue = tie(mine, kept)
        e[b], parts[b], later, sent = pl.pallas_call(
            functools.partial(grad_kernel, [len(arrays)]),
            grid_spec=pltpu.PrefetchScalarGridSpec(
                num_scalar_prefetch=1,
                grid=(width // cover,),
                in_specs=[
                    pl.BlockSpec((two, 8, BLK), lambda n, o, b=b: (n, 0, b)),
                    pl.BlockSpec((BLK, cover), lambda n, o, b=b: (b, n)),
                    pl.BlockSpec((BLK, cover), lambda n, o, b=b: (b, n)),
                ]
                + [pl.BlockSpec((BLK, depth), lambda n, o, at=at: (at, 0)) for _, at in arrays]
                + [pl.BlockSpec((depth, cover), lambda n, o: (o[size - 1], n)), pair_state],
                out_specs=[pl.BlockSpec((BLK, cover), lambda n, o: (0, n))] + [pair_state] * 3,
            ),
            out_shape=[shape((BLK, width), BF16), state_f32, state_f32, shape((heads, DK, DK), BF16)],
            compiler_params=PARAMS,
            cost_estimate=LIGHT,
            name="grad_mixed_rows",
        )(queue, factors, query, early, *[x for x, _ in arrays], full_weight, later)
        if b == 0:
            back = Scan(later, fwd_own[:, :1], sent, True, scan.known)
            back.send_pair()
        order_after = e[b]
        if b:
            part = dot(tie(block, e[b]), mixed[start:end], 0, 0)
            part = part if n == 0 else product.astype(F32) + part
            product = part.astype(BF16)
            order_after = product
        else:
            held = joined(kept, got, e[b])
            last_tree = Tree(held, targets(size - 1), [group_bits[::-1], group_bits])
            last_tree.send()
            order_after = back.take_pair(held[0])
            back.send_all()
        own_rows = pl.BlockSpec((BLK, many * DK), lambda h, b=b: (b, h))
        filled = pl.pallas_call(
            back_kernel,
            grid=(heads // many,),
            in_specs=[pl.BlockSpec((many, 8, BLK), lambda h, b=b: (h, 0, b))]
            + [own_rows] * 3
            + [
                pl.BlockSpec((BLK, many * DK), lambda h: (0, h)),
                pl.BlockSpec((many, 1, weight_rows, half), lambda h, b=b: (h, b, 0, 0)),
                pl.BlockSpec((many, 1, DK, DK), lambda h, b=b: (h, b, 0, 0)),
            ]
            + [pl.BlockSpec(memory_space=pl.ANY)] * len(filled),
            out_specs=[own_rows] * 3,
            out_shape=[rows_bf16] * 3,
            input_output_aliases={7 + m: m for m in range(len(filled))},
            compiler_params=PARAMS,
            cost_estimate=LIGHT,
            name="block_gradients",
        )(tie(factors, order_after), query, key, value, e[b], weights, states, *filled)
        after = [filled[0], product]
    dq, dk_part, dv_part = filled
    grad_in = back.take_all(dq)
    for _ in group_bits[1:]:
        last_tree.take(dq)
        last_tree.send()
    pair_rows = pl.BlockSpec((tok, cover), lambda n: (0, n))
    dk, dv = pl.pallas_call(
        finish_kernel,
        grid=(heads // two,),
        in_specs=[pl.BlockSpec((two, 8, tok), lambda n: (n, 0, 0))]
        + [pair_rows] * 4
        + [pl.BlockSpec((two, DK, DK), lambda n: (n, 0, 0))] * (1 + blocks),
        out_specs=[pair_rows] * 2,
        out_shape=[rows_bf16] * 2,
        compiler_params=PARAMS,
        cost_estimate=LIGHT,
        name="carried_gradients",
    )(
        factors,
        key,
        value,
        dk_part,
        dv_part,
        grad_in,
        *[parts[b] for b in range(blocks)],
    )
    done = [x.astype(F32) + tie(y, dk).astype(F32) for x, y in zip(last_tree.now, last_tree.got)]
    done = jnp.concatenate(done, axis=1)
    grad_weight = most.astype(F32) + jnp.where(mine[size - 1] == place // group, done, 0.0)
    return dq, dk, dv, grad_weight


def solution(mesh):
    both = P("tm", "head")
    return jax.shard_map(
        per_device,
        mesh=mesh,
        in_specs=(both, both, both, both, both, P("head"), P("head", "tm")),
        out_specs=(both, both, both, both),
        check_vma=False,
    )
```
